512 devices in a mesh: row: 8 (over x, y_hi), col: 16 (over z), pipe: 4 (over y_lo, core).
Axes of the slice: x: 4, y: 4 (y_hi: 2, y_lo: 2; y = y_hi * 2 + y_lo), z: 16, core: 2. Of those that a mesh axis runs over, the one named last changes fastest.
Arguments:
- inputs: bfloat16 [1024, 12288], P('col', ('row', 'pipe')), may hold values from -6 to 6
- weight: bfloat16 [12288, 49152], P(('row', 'pipe'), 'col'), may hold values from -0.0546875 to 0.0546875
- upstream: bfloat16 [1024, 49152], P(('row', 'pipe'), 'col'), may hold values from -1.5 to 1.5
- preactivation: bfloat16 [1024, 49152], P(('row', 'pipe'), 'col'), may hold values from -6 to 6
Outputs:
- input_gradient: bfloat16 [1024, 12288], P('col', ('row', 'pipe'))
- weight_gradient: bfloat16 [12288, 49152], P(('row', 'pipe'), 'col')
The draws below stay inside these ranges and needn't reach their ends.
All inputs are finite; a program needn't handle non-finite values.
Results may differ from the reference program's by a relative error of at most 0.0049.
Values may be sent and summed in bfloat16 or wider, within the bound.
No kernel may reach another device: no remote copies, remote signals or barrier semaphores. Data moves between devices by JAX's collectives and lax.ppermute only.
A program may use at most 64 MiB of HBM per device.

```python
import math
import jax
import jax.numpy as jnp
from jax import lax

D = 12288
FF = 49152
TOKENS = 1024


def shard_levels(own_key, extent, pieces, low, top_value):
    factor_of, own = 1.0, jax.random.fold_in(own_key, 6)
    for axis_at, parts in pieces:
        steps = jnp.exp(jax.random.uniform(jax.random.fold_in(own, axis_at), (parts,), jnp.float32, low / len(pieces), top_value / len(pieces)))
        factor_of = factor_of * jnp.repeat(steps, extent[axis_at] // parts).reshape([-1 if axis == axis_at else 1 for axis in range(len(extent))])
    return factor_of


def bell_draw(own_key, shape, width, limit, split=(), kind=jnp.bfloat16):
    array = jax.random.normal(own_key, shape, jnp.float32) * width
    if len(split) > 0:
        array = shard_levels(own_key, shape, split, -0.22, 0.18) * array
    return jnp.clip(array, min=-limit, max=limit).astype(kind)


def setup_inputs(seed: int = 0) -> dict:
    keys = jax.random.split(jax.random.key(seed), 5)
    return {
        "inputs": bell_draw(keys[0], (TOKENS, D), 1.0, 6.0, ((0, 16), (1, 32))),
        "weight": bell_draw(keys[1], (D, FF), D ** -0.5, 0.0546875, ((0, 32), (1, 16))),
        "upstream": bell_draw(keys[2], (TOKENS, FF), 0.25, 1.5, ((0, 32), (1, 16))),
        "preactivation": bell_draw(keys[3], (TOKENS, FF), 1.5, 6.0, ((0, 32), (1, 16))),
    }


gelu_scale = math.sqrt(2.0 / math.pi)
cubic_term = 0.044715

def gelu_slope(values):
    inner = gelu_scale * (values + cubic_term * values * values * values)
    tangent = jnp.tanh(inner)
    return 0.5 * (1.0 + tangent) + 0.5 * values * (1.0 - tangent * tangent) * gelu_scale * (1.0 + 3.0 * cubic_term * values * values)

def reference(inputs, weight, upstream, preactivation):
    slope = gelu_slope(preactivation.astype(jnp.float32))
    hidden_gradient = (upstream.astype(jnp.float32) * slope).astype(jnp.bfloat16)
    input_gradient = lax.dot_general(hidden_gradient, weight, (((1,), (1,)), ((), ())), preferred_element_type=jnp.float32).astype(jnp.bfloat16)
    weight_gradient = lax.dot_general(inputs, hidden_gradient, (((0,), (0,)), ((), ())), preferred_element_type=jnp.float32).astype(jnp.bfloat16)
    return (input_gradient, weight_gradient)
```

```python
import math

import jax
import jax.numpy as jnp
from jax import lax
from jax.experimental import pallas as pl
from jax.experimental.pallas import tpu as pltpu
from jax.sharding import Mesh
from jax.sharding import PartitionSpec as P

gelu_scale = math.sqrt(2.0 / math.pi)
cubic_term = 0.044715

MIB = 1024 * 1024
PLANE = ("x", "yh", "yl", "core")
Z = ("zh", "zl")
ROWS_BY_ROWS = (((1,), (1,)), ((), ()))


def gelu_slope(values):
    inner = gelu_scale * (values + cubic_term * values * values * values)
    tangent = jnp.tanh(inner)
    return 0.5 * (1.0 + tangent) + 0.5 * values * (1.0 - tangent * tangent) * gelu_scale * (
        1.0 + 3.0 * cubic_term * values * values
    )


def vmem():
    return pl.BlockSpec(memory_space=pltpu.VMEM)


def smem():
    return pl.BlockSpec(memory_space=pltpu.SMEM)


def chip_number(info_ref, first, second):
    core = info_ref[3]
    return first * (4 - 3 * core) + second * (1 + 3 * core)


def block_rows(k):
    return pl.ds(pl.multiple_of(k * 32, 32), 32)


def early_kernel(l0_ref, l1_ref, l3_ref, w_own_ref, w_sib_ref, out_ref, left):
    for j, ref in enumerate((l0_ref, l1_ref, l3_ref)):
        for i in range(4):
            left[pl.ds(j * 128 + i * 32, 32), :] = ref[i]
    for n, w_ref in enumerate((w_own_ref, w_sib_ref)):
        out_ref[:, n * 384 : (n + 1) * 384] = lax.dot_general(
            left[...], w_ref[...], ROWS_BY_ROWS, preferred_element_type=jnp.float32
        )


def early_sums(lines, w_own, w_sib):
    return pl.pallas_call(
        early_kernel,
        out_shape=jax.ShapeDtypeStruct((384, 768), jnp.float32),
        in_specs=[vmem()] * 5,
        out_specs=vmem(),
        scratch_shapes=[pltpu.VMEM((384, 3072), jnp.bfloat16)],
        compiler_params=pltpu.CompilerParams(vmem_limit_bytes=24 * MIB),
        cost_estimate=pl.CostEstimate(
            flops=2 * 384 * 3072 * 768, bytes_accessed=8 * MIB, transcendentals=0
        ),
        name="early_sums",
    )(*lines, w_own, w_sib)


def late_kernel(info_ref, l0_ref, l1_ref, l3_ref, l2_ref, early_ref, w_own_ref, w_sib_ref, own_ref, s1_ref, s2_ref, s3_ref, plane_ref, left, acc):
    for i in range(4):
        left[pl.ds(i * 32, 32), :] = l2_ref[i]
    second = info_ref[2]
    for n, w_ref in enumerate((w_own_ref, w_sib_ref)):
        total = lax.dot_general(
            left[...], w_ref[...], ROWS_BY_ROWS, preferred_element_type=jnp.float32
        )
        for i in range(4):
            k = chip_number(info_ref, i, lax.rem(second + 2, 4))
            acc[block_rows(k), n * 384 : (n + 1) * 384] = total[i * 32 : (i + 1) * 32]
    for i in range(4):
        k = chip_number(info_ref, i, lax.rem(second + 2, 4))
        plane_ref[block_rows(k), :] = l2_ref[i]
        for j, (d, ref) in enumerate(((0, l0_ref), (1, l1_ref), (3, l3_ref))):
            k = chip_number(info_ref, i, lax.rem(second + d, 4))
            acc[block_rows(k), :] = early_ref[j * 128 + i * 32 : j * 128 + (i + 1) * 32, :]
            plane_ref[block_rows(k), :] = ref[i]
    for d, out in enumerate((own_ref, s1_ref, s2_ref, s3_ref)):
        residue = lax.rem(info_ref[0] + d, 4)
        for x in range(4):
            out[x] = acc[block_rows(x * 4 + residue), :].astype(out.dtype)


def late_sums(info, lines, far, early, w_own, w_sib):
    shape = (4, 32, 768)
    return pl.pallas_call(
        late_kernel,
        out_shape=[jax.ShapeDtypeStruct(shape, jnp.float32)]
        + [jax.ShapeDtypeStruct(shape, jnp.bfloat16)] * 3
        + [jax.ShapeDtypeStruct((512, 3072), jnp.bfloat16)],
        in_specs=[smem()] + [vmem()] * 7,
        out_specs=[vmem()] * 5,
        scratch_shapes=[
            pltpu.VMEM((128, 3072), jnp.bfloat16),
            pltpu.VMEM((512, 768), jnp.float32),
        ],
        compiler_params=pltpu.CompilerParams(vmem_limit_bytes=28 * MIB),
        cost_estimate=pl.CostEstimate(
            flops=2 * 128 * 3072 * 768, bytes_accessed=8 * MIB, transcendentals=0
        ),
        name="late_sums",
    )(info, *lines, far, early, w_own, w_sib)


def stage_kernel(info_ref, own_ref, r1_ref, r2_ref, r3_ref, o_ref, s1_ref, s2_ref, s3_ref):
    zh = info_ref[0] // 4
    for d, out in enumerate((o_ref, s1_ref, s2_ref, s3_ref)):
        i = lax.rem(zh + d, 4)
        total = own_ref[i]
        for r in (r1_ref, r2_ref, r3_ref):
            total = total + r[i].astype(jnp.float32)
        out[...] = total.astype(out.dtype)


def stage_sums(info, own, received):
    shape = (32, 768)
    return pl.pallas_call(
        stage_kernel,
        out_shape=[jax.ShapeDtypeStruct(shape, jnp.float32)]
        + [jax.ShapeDtypeStruct(shape, jnp.bfloat16)] * 3,
        in_specs=[smem()] + [vmem()] * 4,
        out_specs=[vmem()] * 4,
        compiler_params=pltpu.CompilerParams(vmem_limit_bytes=16 * MIB),
        cost_estimate=pl.CostEstimate(flops=400000, bytes_accessed=2 * MIB, transcendentals=0),
        name="stage_sums",
    )(info, own, *received)


def final_kernel(own_ref, r1_ref, r2_ref, r3_ref, o_ref, s_ref):
    total = own_ref[...]
    for r in (r1_ref, r2_ref, r3_ref):
        total = total + r[...].astype(jnp.float32)
    o_ref[...] = total[:, :384].astype(jnp.bfloat16)
    s_ref[...] = total[:, 384:].astype(jnp.bfloat16)


def final_sums(own, received):
    shape = jax.ShapeDtypeStruct((32, 384), jnp.bfloat16)
    return pl.pallas_call(
        final_kernel,
        out_shape=[shape, shape],
        in_specs=[vmem()] * 4,
        out_specs=[vmem()] * 2,
        compiler_params=pltpu.CompilerParams(vmem_limit_bytes=4 * MIB),
        cost_estimate=pl.CostEstimate(flops=100000, bytes_accessed=MIB // 4, transcendentals=0),
        name="final_sums",
    )(own, *received)


def weight_kernel(info_ref, in_ref, own_ref, sib_ref, out_ref, left):

    @pl.when(pl.program_id(0) == 0)
    def _():
        core = info_ref[3]
        for which in range(2):
            half = core if which == 0 else 1 - core
            rows = [
                in_ref[pl.ds(pl.multiple_of(k * 64 + half * 32, 32), 32), :] for k in range(16)
            ]
            block = jnp.concatenate(rows, axis=0)
            left[:, which * 512 : (which + 1) * 512] = block.T

    total = jnp.dot(left[:, :512], own_ref[...], preferred_element_type=jnp.float32)
    total += jnp.dot(left[:, 512:], sib_ref[...], preferred_element_type=jnp.float32)
    out_ref[...] = total.astype(jnp.bfloat16)


def weight_sums(info, gathered, hg_own, hg_sib):
    tile = 512
    return pl.pallas_call(
        weight_kernel,
        out_shape=jax.ShapeDtypeStruct((384, 3072), jnp.bfloat16),
        grid_spec=pltpu.PrefetchScalarGridSpec(
            num_scalar_prefetch=1,
            grid=(3072 // tile,),
            in_specs=[
                pl.BlockSpec((1024, 384), lambda j, info: (0, 0)),
                pl.BlockSpec((512, tile), lambda j, info: (0, j)),
                pl.BlockSpec((512, tile), lambda j, info: (0, j)),
            ],
            out_specs=pl.BlockSpec((384, tile), lambda j, info: (0, j)),
            scratch_shapes=[pltpu.VMEM((384, 1024), jnp.bfloat16)],
        ),
        compiler_params=pltpu.CompilerParams(vmem_limit_bytes=24 * MIB),
        cost_estimate=pl.CostEstimate(
            flops=2 * 1024 * 3072 * 384, bytes_accessed=10 * MIB, transcendentals=0
        ),
        name="weight_sums",
    )(info, gathered, hg_own, hg_sib)


def plane_shift(first, by):
    pairs = []
    for x in range(4):
        for y in range(4):
            for core in range(2):
                along_x = (core == 0) == first
                to = ((x + by) % 4, y) if along_x else (x, (y + by) % 4)
                pairs.append(((x * 4 + y) * 2 + core, (to[0] * 4 + to[1]) * 2 + core))
    return pairs


def column_shift(by):
    return [(z * 2 + c, (z + by[c]) % 16 * 2 + c) for z in range(16) for c in range(2)]


def first_axis_groups():
    place = [[[(x * 4 + y) * 2 + c for c in range(2)] for y in range(4)] for x in range(4)]
    along_x = [[place[i][j][0] for i in range(4)] for j in range(4)]
    along_y = [[place[j][i][1] for i in range(4)] for j in range(4)]
    return along_x + along_y


def per_device(inputs, weight, upstream, preactivation):
    core = lax.axis_index("core")
    x, y, z = lax.axis_index("x"), lax.axis_index(("yh", "yl")), lax.axis_index(Z)
    first, second = jnp.where(core == 0, x, y), jnp.where(core == 0, y, x)
    info = jnp.stack([z, first, second, core]).astype(jnp.int32)
    swap = [(0, 1), (1, 0)]

    slope = gelu_slope(preactivation.astype(jnp.float32))
    local = (upstream.astype(jnp.float32) * slope).astype(jnp.bfloat16)
    line = lax.all_gather(
        local, PLANE, axis=0, tiled=True, axis_index_groups=first_axis_groups()
    ).reshape(4, 32, 3072)
    weight_then, inputs, line = lax.optimization_barrier((weight, inputs, line))
    w_sib = lax.ppermute(weight_then, "core", swap)
    far = lax.ppermute(line, PLANE, plane_shift(False, -2))
    line1 = lax.ppermute(line, PLANE, plane_shift(False, -1))
    line3 = lax.ppermute(line, PLANE, plane_shift(False, 1))
    gathered = lax.all_gather(inputs, Z, axis=0, tiled=True)
    far, line1, line3, gathered = lax.optimization_barrier((far, line1, line3, gathered))
    lines = (line, line1, line3)
    early = early_sums(lines, weight, w_sib)

    own, *sends, hg_own = late_sums(info, lines, far, early, weight, w_sib)
    received = [
        lax.ppermute(s, Z + ("core",), column_shift(by))
        for s, by in zip(sends, ((1, 1), (2, -2), (-1, -1)))
    ]
    *received, hg_own = lax.optimization_barrier((*received, hg_own))
    hg_sib = lax.ppermute(hg_own, "core", swap)
    own, *sends = stage_sums(info, own, received)
    received = [
        lax.ppermute(s, Z, [(i, (i + 4 * (d + 1)) % 16) for i in range(16)])
        for d, s in enumerate(sends)
    ]
    weight_total = weight_sums(info, gathered, hg_own, hg_sib)
    weight_total, *received = lax.optimization_barrier((weight_total, *received))
    mine, other = final_sums(own, received)
    other = lax.ppermute(other, "core", swap)
    input_gradient = jnp.concatenate(
        [jnp.where(core == 0, mine, other), jnp.where(core == 0, other, mine)], axis=0
    )
    return (input_gradient, weight_total)


def solution(mesh):
    fine = Mesh(
        mesh.devices.reshape(4, 2, 4, 4, 2, 2), ("x", "yh", "zh", "zl", "yl", "core")
    )
    in_specs = (P(Z, PLANE), P(PLANE, Z), P(PLANE, Z), P(PLANE, Z))
    out_specs = (P(Z, PLANE), P(PLANE, Z))
    return jax.shard_map(
        per_device, mesh=fine, in_specs=in_specs, out_specs=out_specs, check_vma=False
    )
```

```python
import math

import jax
import jax.numpy as jnp
from jax import lax
from jax.experimental import pallas as pl
from jax.experimental.pallas import tpu as pltpu
from jax.sharding import Mesh
from jax.sharding import PartitionSpec as P

gelu_scale = math.sqrt(2.0 / math.pi)
cubic_term = 0.044715

MIB = 1024 * 1024
PLANE = ("x", "yh", "yl", "core")
Z = ("zh", "zl")
ROWS_BY_ROWS = (((1,), (1,)), ((), ()))


def gelu_slope(values):
    inner = gelu_scale * (values + cubic_term * values * values * values)
    tangent = jnp.tanh(inner)
    return 0.5 * (1.0 + tangent) + 0.5 * values * (1.0 - tangent * tangent) * gelu_scale * (
        1.0 + 3.0 * cubic_term * values * values
    )


def vmem():
    return pl.BlockSpec(memory_space=pltpu.VMEM)


def smem():
    return pl.BlockSpec(memory_space=pltpu.SMEM)


def chip_number(info_ref, first, second):
    core = info_ref[3]
    return first * (4 - 3 * core) + second * (1 + 3 * core)


def block_rows(k):
    return pl.ds(pl.multiple_of(k * 32, 32), 32)


def partial_kernel(info_ref, l0_ref, l1_ref, l2_ref, l3_ref, w_own_ref, w_sib_ref, own_ref, s1_ref, s2_ref, s3_ref, plane_ref, plane, w, acc, sems):
    second = info_ref[2]
    copies = []
    for d, ref in enumerate((l0_ref, l1_ref, l2_ref, l3_ref)):
        for i in range(4):
            k = chip_number(info_ref, i, lax.rem(second + d, 4))
            copies.append(
                pltpu.make_async_copy(ref.at[i], plane.at[block_rows(k), :], sems.at[d * 4 + i])
            )
    weights = [
        pltpu.make_async_copy(ref, w.at[n], sems.at[16 + n])
        for n, ref in enumerate((w_own_ref, w_sib_ref))
    ]
    for copy in copies + weights:
        copy.start()
    for copy in copies:
        copy.wait()
    result = pltpu.make_async_copy(plane, plane_ref, sems.at[18])
    result.start()
    for n, copy in enumerate(weights):
        copy.wait()
        acc[:, n * 384 : (n + 1) * 384] = lax.dot_general(
            plane[...], w[n], ROWS_BY_ROWS, preferred_element_type=jnp.float32
        )
    result.wait()
    for d, out in enumerate((own_ref, s1_ref, s2_ref, s3_ref)):
        residue = lax.rem(info_ref[0] + d, 4)
        for x in range(4):
            out[x] = acc[block_rows(x * 4 + residue), :].astype(out.dtype)


def partial_sums(info, lines, w_own, w_sib):
    shape = (4, 32, 768)
    return pl.pallas_call(
        partial_kernel,
        out_shape=[jax.ShapeDtypeStruct(shape, jnp.float32)]
        + [jax.ShapeDtypeStruct(shape, jnp.bfloat16)] * 3
        + [jax.ShapeDtypeStruct((512, 3072), jnp.bfloat16)],
        in_specs=[smem()] + [pl.BlockSpec(memory_space=pl.ANY)] * 6,
        out_specs=[vmem()] * 4 + [pl.BlockSpec(memory_space=pl.ANY)],
        scratch_shapes=[
            pltpu.VMEM((512, 3072), jnp.bfloat16),
            pltpu.VMEM((2, 384, 3072), jnp.bfloat16),
            pltpu.VMEM((512, 768), jnp.float32),
            pltpu.SemaphoreType.DMA((19,)),
        ],
        compiler_params=pltpu.CompilerParams(vmem_limit_bytes=52 * MIB),
        cost_estimate=pl.CostEstimate(
            flops=2 * 512 * 3072 * 768, bytes_accessed=8 * MIB, transcendentals=0
        ),
        name="partial_sums",
    )(info, *lines, w_own, w_sib)


def stage_kernel(info_ref, own_ref, r1_ref, r2_ref, r3_ref, o_ref, s1_ref, s2_ref, s3_ref):
    zh = info_ref[0] // 4
    for d, out in enumerate((o_ref, s1_ref, s2_ref, s3_ref)):
        i = lax.rem(zh + d, 4)
        total = own_ref[i]
        for r in (r1_ref, r2_ref, r3_ref):
            total = total + r[i].astype(jnp.float32)
        out[...] = total.astype(out.dtype)


def stage_sums(info, own, received):
    shape = (32, 768)
    return pl.pallas_call(
        stage_kernel,
        out_shape=[jax.ShapeDtypeStruct(shape, jnp.float32)]
        + [jax.ShapeDtypeStruct(shape, jnp.bfloat16)] * 3,
        in_specs=[smem()] + [vmem()] * 4,
        out_specs=[vmem()] * 4,
        compiler_params=pltpu.CompilerParams(vmem_limit_bytes=16 * MIB),
        cost_estimate=pl.CostEstimate(flops=400000, bytes_accessed=2 * MIB, transcendentals=0),
        name="stage_sums",
    )(info, own, *received)


def final_kernel(own_ref, r1_ref, r2_ref, r3_ref, o_ref, s_ref):
    total = own_ref[...]
    for r in (r1_ref, r2_ref, r3_ref):
        total = total + r[...].astype(jnp.float32)
    o_ref[...] = total[:, :384].astype(jnp.bfloat16)
    s_ref[...] = total[:, 384:].astype(jnp.bfloat16)


def final_sums(own, received):
    shape = jax.ShapeDtypeStruct((32, 384), jnp.bfloat16)
    return pl.pallas_call(
        final_kernel,
        out_shape=[shape, shape],
        in_specs=[vmem()] * 4,
        out_specs=[vmem()] * 2,
        compiler_params=pltpu.CompilerParams(vmem_limit_bytes=4 * MIB),
        cost_estimate=pl.CostEstimate(flops=100000, bytes_accessed=MIB // 4, transcendentals=0),
        name="final_sums",
    )(own, *received)


def weight_kernel(info_ref, n0_ref, n1_ref, n2_ref, n3_ref, own_ref, sib_ref, out_ref, tokens, left):

    @pl.when(pl.program_id(0) == 0)
    def _():
        z, core = info_ref[0], info_ref[3]
        for ref, far in ((n0_ref, 0), (n1_ref, -1), (n2_ref, 4 * core - 2), (n3_ref, 1)):
            for e in range(4):
                k = lax.rem(z + far + 4 * e + 16, 16)
                for which in range(2):
                    half = core if which == 0 else 1 - core
                    rows = pl.ds(pl.multiple_of(which * 512 + k * 32, 32), 32)
                    tokens[rows, :] = ref[e, pl.ds(pl.multiple_of(half * 32, 32), 32), :]
        left[...] = tokens[...].T

    total = jnp.dot(left[:, :512], own_ref[...], preferred_element_type=jnp.float32)
    total += jnp.dot(left[:, 512:], sib_ref[...], preferred_element_type=jnp.float32)
    out_ref[...] = total.astype(jnp.bfloat16)


def weight_sums(info, near, hg_own, hg_sib):
    tile = 512
    return pl.pallas_call(
        weight_kernel,
        out_shape=jax.ShapeDtypeStruct((384, 3072), jnp.bfloat16),
        grid_spec=pltpu.PrefetchScalarGridSpec(
            num_scalar_prefetch=1,
            grid=(3072 // tile,),
            in_specs=[pl.BlockSpec((4, 64, 384), lambda j, info: (0, 0, 0))] * 4
            + [pl.BlockSpec((512, tile), lambda j, info: (0, j))] * 2,
            out_specs=pl.BlockSpec((384, tile), lambda j, info: (0, j)),
            scratch_shapes=[
                pltpu.VMEM((1024, 384), jnp.bfloat16),
                pltpu.VMEM((384, 1024), jnp.bfloat16),
            ],
        ),
        compiler_params=pltpu.CompilerParams(vmem_limit_bytes=24 * MIB),
        cost_estimate=pl.CostEstimate(
            flops=2 * 1024 * 3072 * 384, bytes_accessed=10 * MIB, transcendentals=0
        ),
        name="weight_sums",
    )(info, *near, hg_own, hg_sib)


def plane_shift(first, by):
    pairs = []
    for x in range(4):
        for y in range(4):
            for core in range(2):
                along_x = (core == 0) == first
                to = ((x + by) % 4, y) if along_x else (x, (y + by) % 4)
                pairs.append(((x * 4 + y) * 2 + core, (to[0] * 4 + to[1]) * 2 + core))
    return pairs


def far_shift(by):
    return [(z, (z + 4 * by) % 16) for z in range(16)]


def column_shift(by):
    return [(z * 2 + c, (z + by[c]) % 16 * 2 + c) for z in range(16) for c in range(2)]


def first_axis_groups():
    place = [[[(x * 4 + y) * 2 + c for c in range(2)] for y in range(4)] for x in range(4)]
    along_x = [[place[i][j][0] for i in range(4)] for j in range(4)]
    along_y = [[place[j][i][1] for i in range(4)] for j in range(4)]
    return along_x + along_y


NEAR = ((1, 1), (2, -2), (-1, -1))


def per_device(inputs, weight, upstream, preactivation):
    core = lax.axis_index("core")
    x, y, z = lax.axis_index("x"), lax.axis_index(("yh", "yl")), lax.axis_index(Z)
    first, second = jnp.where(core == 0, x, y), jnp.where(core == 0, y, x)
    info = jnp.stack([z, first, second, core]).astype(jnp.int32)
    swap = [(0, 1), (1, 0)]

    slope = gelu_slope(preactivation.astype(jnp.float32))
    local = (upstream.astype(jnp.float32) * slope).astype(jnp.bfloat16)
    line = lax.all_gather(
        local, PLANE, axis=0, tiled=True, axis_index_groups=first_axis_groups()
    ).reshape(4, 32, 3072)
    weight_then, line = lax.optimization_barrier((weight, line))
    w_sib = lax.ppermute(weight_then, "core", swap)
    inputs, w_sib = lax.optimization_barrier((inputs, w_sib))
    lines = [line] + [lax.ppermute(line, PLANE, plane_shift(False, -d)) for d in (1, 2, 3)]
    near = [inputs] + [lax.ppermute(inputs, Z, far_shift(-d)) for d in (1, 2)]
    inputs, near[1] = lax.optimization_barrier((inputs, near[1]))
    last = lax.ppermute(inputs, Z, far_shift(-3))
    lines, near = lax.optimization_barrier((lines, near))
    near = near + [last]

    own, *sends, hg_own = partial_sums(info, lines, weight, w_sib)
    own, near = lax.optimization_barrier((own, near))
    near, hg_own = lax.optimization_barrier((jnp.stack(near), hg_own))
    nears = [near] + [lax.ppermute(near, Z + ("core",), column_shift(by)) for by in NEAR]
    received = [
        lax.ppermute(s, Z + ("core",), column_shift(by)) for s, by in zip(sends, NEAR)
    ]
    hg_sib = lax.ppermute(hg_own, "core", swap)
    own, *sends = stage_sums(info, own, received)
    received = [
        lax.ppermute(s, Z, far_shift(d + 1))
        for d, s in enumerate(sends)
    ]
    weight_total = weight_sums(info, nears, hg_own, hg_sib)
    weight_total, *received = lax.optimization_barrier((weight_total, *received))
    mine, other = final_sums(own, received)
    other = lax.ppermute(other, "core", swap)
    input_gradient = jnp.concatenate(
        [jnp.where(core == 0, mine, other), jnp.where(core == 0, other, mine)], axis=0
    )
    return (input_gradient, weight_total)


def solution(mesh):
    fine = Mesh(
        mesh.devices.reshape(4, 2, 4, 4, 2, 2), ("x", "yh", "zh", "zl", "yl", "core")
    )
    in_specs = (P(Z, PLANE), P(PLANE, Z), P(PLANE, Z), P(PLANE, Z))
    out_specs = (P(Z, PLANE), P(PLANE, Z))
    return jax.shard_map(
        per_device, mesh=fine, in_specs=in_specs, out_specs=out_specs, check_vma=False
    )
```

```python
import math

import jax
import jax.numpy as jnp
from jax import lax
from jax.experimental import pallas as pl
from jax.experimental.pallas import tpu as pltpu
from jax.sharding import Mesh
from jax.sharding import PartitionSpec as P

gelu_scale = math.sqrt(2.0 / math.pi)
cubic_term = 0.044715

MIB = 1024 * 1024
PLANE = ("x", "yh", "yl", "core")
Z = ("zh", "zl")
ROWS_BY_ROWS = (((1,), (1,)), ((), ()))


def gelu_slope(values):
    inner = gelu_scale * (values + cubic_term * values * values * values)
    tangent = jnp.tanh(inner)
    return 0.5 * (1.0 + tangent) + 0.5 * values * (1.0 - tangent * tangent) * gelu_scale * (
        1.0 + 3.0 * cubic_term * values * values
    )


def vmem():
    return pl.BlockSpec(memory_space=pltpu.VMEM)


def smem():
    return pl.BlockSpec(memory_space=pltpu.SMEM)


def chip_number(info_ref, first, second):
    core = info_ref[3]
    return first * (4 - 3 * core) + second * (1 + 3 * core)


def block_rows(k):
    return pl.ds(pl.multiple_of(k * 32, 32), 32)


def partial_kernel(info_ref, l0_ref, l1_ref, l2_ref, l3_ref, w_own_ref, w_sib_ref, own_ref, s1_ref, s2_ref, s3_ref, plane_ref, plane, w, acc, sems):
    second = info_ref[2]
    copies = []
    for d, ref in enumerate((l0_ref, l1_ref, l2_ref, l3_ref)):
        for i in range(4):
            k = chip_number(info_ref, i, lax.rem(second + d, 4))
            copies.append(
                pltpu.make_async_copy(ref.at[i], plane.at[block_rows(k), :], sems.at[d * 4 + i])
            )
    weights = [
        pltpu.make_async_copy(ref, w.at[n], sems.at[16 + n])
        for n, ref in enumerate((w_own_ref, w_sib_ref))
    ]
    for copy in copies + weights:
        copy.start()
    for copy in copies:
        copy.wait()
    result = pltpu.make_async_copy(plane, plane_ref, sems.at[18])
    result.start()
    for n, copy in enumerate(weights):
        copy.wait()
        acc[:, n * 384 : (n + 1) * 384] = lax.dot_general(
            plane[...], w[n], ROWS_BY_ROWS, preferred_element_type=jnp.float32
        )
    result.wait()
    for d, out in enumerate((own_ref, s1_ref, s2_ref, s3_ref)):
        residue = lax.rem(info_ref[0] + d, 4)
        for x in range(4):
            out[x] = acc[block_rows(x * 4 + residue), :].astype(out.dtype)


def partial_sums(info, lines, w_own, w_sib):
    shape = (4, 32, 768)
    return pl.pallas_call(
        partial_kernel,
        out_shape=[jax.ShapeDtypeStruct(shape, jnp.float32)]
        + [jax.ShapeDtypeStruct(shape, jnp.bfloat16)] * 3
        + [jax.ShapeDtypeStruct((512, 3072), jnp.bfloat16)],
        in_specs=[smem()] + [pl.BlockSpec(memory_space=pl.ANY)] * 6,
        out_specs=[vmem()] * 4 + [pl.BlockSpec(memory_space=pl.ANY)],
        scratch_shapes=[
            pltpu.VMEM((512, 3072), jnp.bfloat16),
            pltpu.VMEM((2, 384, 3072), jnp.bfloat16),
            pltpu.VMEM((512, 768), jnp.float32),
            pltpu.SemaphoreType.DMA((19,)),
        ],
        compiler_params=pltpu.CompilerParams(vmem_limit_bytes=52 * MIB),
        cost_estimate=pl.CostEstimate(
            flops=2 * 512 * 3072 * 768, bytes_accessed=8 * MIB, transcendentals=0
        ),
        name="partial_sums",
    )(info, *lines, w_own, w_sib)


def stage_kernel(info_ref, own_ref, r1_ref, r2_ref, r3_ref, out_ref):
    core = info_ref[3]
    for i in range(4):
        total = own_ref[i]
        for r in (r1_ref, r2_ref, r3_ref):
            total = total + r[i].astype(jnp.float32)
        total = total.astype(jnp.bfloat16)
        out_ref[i, core] = total[:, :384]
        out_ref[i, 1 - core] = total[:, 384:]


def stage_sums(info, own, received):
    return pl.pallas_call(
        stage_kernel,
        out_shape=jax.ShapeDtypeStruct((4, 2, 32, 384), jnp.bfloat16),
        in_specs=[smem()] + [vmem()] * 4,
        out_specs=vmem(),
        compiler_params=pltpu.CompilerParams(vmem_limit_bytes=8 * MIB),
        cost_estimate=pl.CostEstimate(flops=400000, bytes_accessed=MIB, transcendentals=0),
        name="stage_sums",
    )(info, own, *received)


def weight_kernel(info_ref, n0_ref, n1_ref, n2_ref, n3_ref, own_ref, sib_ref, out_ref, tokens, left):

    @pl.when(pl.program_id(0) == 0)
    def _():
        z, core = info_ref[0], info_ref[3]
        for d, ref in enumerate((n0_ref, n1_ref, n2_ref, n3_ref)):
            for e in range(4):
                k = 4 * e + lax.rem(z + 4 - d, 4)
                for which in range(2):
                    half = core if which == 0 else 1 - core
                    rows = pl.ds(pl.multiple_of(which * 512 + k * 32, 32), 32)
                    tokens[rows, :] = ref[e, pl.ds(pl.multiple_of(half * 32, 32), 32), :]
        left[...] = tokens[...].T

    total = jnp.dot(left[:, :512], own_ref[...], preferred_element_type=jnp.float32)
    total += jnp.dot(left[:, 512:], sib_ref[...], preferred_element_type=jnp.float32)
    out_ref[...] = total.astype(jnp.bfloat16)


def weight_sums(info, near, hg_own, hg_sib):
    tile = 512
    return pl.pallas_call(
        weight_kernel,
        out_shape=jax.ShapeDtypeStruct((384, 3072), jnp.bfloat16),
        grid_spec=pltpu.PrefetchScalarGridSpec(
            num_scalar_prefetch=1,
            grid=(3072 // tile,),
            in_specs=[pl.BlockSpec((4, 64, 384), lambda j, info: (0, 0, 0))] * 4
            + [pl.BlockSpec((512, tile), lambda j, info: (0, j))] * 2,
            out_specs=pl.BlockSpec((384, tile), lambda j, info: (0, j)),
            scratch_shapes=[
                pltpu.VMEM((1024, 384), jnp.bfloat16),
                pltpu.VMEM((384, 1024), jnp.bfloat16),
            ],
        ),
        compiler_params=pltpu.CompilerParams(vmem_limit_bytes=53 * MIB),
        cost_estimate=pl.CostEstimate(
            flops=2 * 1024 * 3072 * 384, bytes_accessed=10 * MIB, transcendentals=0
        ),
        name="weight_sums",
    )(info, *near, hg_own, hg_sib)


def plane_shift(first, by):
    pairs = []
    for x in range(4):
        for y in range(4):
            for core in range(2):
                along_x = (core == 0) == first
                to = ((x + by) % 4, y) if along_x else (x, (y + by) % 4)
                pairs.append(((x * 4 + y) * 2 + core, (to[0] * 4 + to[1]) * 2 + core))
    return pairs


def column_shift(by):
    return [(z * 2 + c, (z + by[c]) % 16 * 2 + c) for z in range(16) for c in range(2)]


def first_axis_groups():
    place = [[[(x * 4 + y) * 2 + c for c in range(2)] for y in range(4)] for x in range(4)]
    along_x = [[place[i][j][0] for i in range(4)] for j in range(4)]
    along_y = [[place[j][i][1] for i in range(4)] for j in range(4)]
    return along_x + along_y


NEAR = ((1, 1), (2, -2), (-1, -1))


def per_device(inputs, weight, upstream, preactivation):
    core = lax.axis_index("core")
    x, y, z = lax.axis_index("x"), lax.axis_index(("yh", "yl")), lax.axis_index(Z)
    first, second = jnp.where(core == 0, x, y), jnp.where(core == 0, y, x)
    info = jnp.stack([z, first, second, core]).astype(jnp.int32)
    swap = [(0, 1), (1, 0)]

    slope = gelu_slope(preactivation.astype(jnp.float32))
    local = (upstream.astype(jnp.float32) * slope).astype(jnp.bfloat16)
    line = lax.all_gather(
        local, PLANE, axis=0, tiled=True, axis_index_groups=first_axis_groups()
    ).reshape(4, 32, 3072)
    weight_then, line = lax.optimization_barrier((weight, line))
    w_sib = lax.ppermute(weight_then, "core", swap)
    inputs, w_sib = lax.optimization_barrier((inputs, w_sib))
    lines = [line] + [lax.ppermute(line, PLANE, plane_shift(False, -d)) for d in (1, 2, 3)]
    near = lax.all_to_all(
        jnp.broadcast_to(inputs[None], (4, 64, 384)), "zh", split_axis=0, concat_axis=0, tiled=True
    )
    lines, near = lax.optimization_barrier((lines, near))

    own, *sends, hg_own = partial_sums(info, lines, weight, w_sib)
    own, near = lax.optimization_barrier((own, near))
    received = [
        lax.ppermute(s, Z + ("core",), column_shift(by)) for s, by in zip(sends, NEAR)
    ]
    nears = [near] + [lax.ppermute(near, Z + ("core",), column_shift(by)) for by in NEAR]
    hg_sib = lax.ppermute(hg_own, "core", swap)
    summed = stage_sums(info, own, received).reshape(8, 32, 384)
    summed = lax.all_to_all(summed, ("zh", "core"), split_axis=0, concat_axis=0, tiled=True)
    weight_total = weight_sums(info, nears, hg_own, hg_sib)
    weight_total, summed = lax.optimization_barrier((weight_total, summed))
    summed = summed.reshape(4, 64, 384).astype(jnp.float32)
    input_gradient = (summed[0] + summed[1] + summed[2] + summed[3]).astype(jnp.bfloat16)
    return (input_gradient, weight_total)


def solution(mesh):
    fine = Mesh(
        mesh.devices.reshape(4, 2, 4, 4, 2, 2), ("x", "yh", "zh", "zl", "yl", "core")
    )
    in_specs = (P(Z, PLANE), P(PLANE, Z), P(PLANE, Z), P(PLANE, Z))
    out_specs = (P(Z, PLANE), P(PLANE, Z))
    return jax.shard_map(
        per_device, mesh=fine, in_specs=in_specs, out_specs=out_specs, check_vma=False
    )
```

```python
import math

import jax
import jax.numpy as jnp
from jax import lax
from jax.experimental import pallas as pl
from jax.experimental.pallas import tpu as pltpu
from jax.sharding import Mesh
from jax.sharding import PartitionSpec as P

gelu_scale = math.sqrt(2.0 / math.pi)
cubic_term = 0.044715

MIB = 1024 * 1024
PLANE = ("x", "yh", "yl", "core")
Z = ("zh", "zl")
ROWS_BY_ROWS = (((1,), (1,)), ((), ()))


def gelu_slope(values):
    inner = gelu_scale * (values + cubic_term * values * values * values)
    tangent = jnp.tanh(inner)
    return 0.5 * (1.0 + tangent) + 0.5 * values * (1.0 - tangent * tangent) * gelu_scale * (
        1.0 + 3.0 * cubic_term * values * values
    )


def vmem():
    return pl.BlockSpec(memory_space=pltpu.VMEM)


def smem():
    return pl.BlockSpec(memory_space=pltpu.SMEM)


def chip_number(info_ref, first, second):
    core = info_ref[3]
    return first * (4 - 3 * core) + second * (1 + 3 * core)


def block_rows(k):
    return pl.ds(pl.multiple_of(k * 32, 32), 32)


def partial_kernel(info_ref, lines_ref, w_own_ref, w_sib_ref, own_ref, s1_ref, s2_ref, s3_ref, plane_ref, w_sib, acc, sems):
    copies = []
    for j in range(4):
        for i in range(4):
            rows = block_rows(chip_number(info_ref, i, j))
            copies.append(
                pltpu.make_async_copy(lines_ref.at[j, i], plane_ref.at[rows, :], sems.at[j * 4 + i])
            )
    weights = pltpu.make_async_copy(w_sib_ref, w_sib, sems.at[16])
    for copy in copies:
        copy.start()
    weights.start()
    for copy in copies:
        copy.wait()
    acc[:, :384] = lax.dot_general(
        plane_ref[...], w_own_ref[...], ROWS_BY_ROWS, preferred_element_type=jnp.float32
    )
    weights.wait()
    acc[:, 384:] = lax.dot_general(
        plane_ref[...], w_sib[...], ROWS_BY_ROWS, preferred_element_type=jnp.float32
    )
    for d, out in enumerate((own_ref, s1_ref, s2_ref, s3_ref)):
        residue = lax.rem(info_ref[0] + d, 4)
        for x in range(4):
            out[x] = acc[block_rows(x * 4 + residue), :].astype(out.dtype)


def partial_sums(info, lines, w_own, w_sib):
    shape = (4, 32, 768)
    return pl.pallas_call(
        partial_kernel,
        out_shape=[jax.ShapeDtypeStruct(shape, jnp.float32)]
        + [jax.ShapeDtypeStruct(shape, jnp.bfloat16)] * 3
        + [jax.ShapeDtypeStruct((512, 3072), jnp.bfloat16)],
        in_specs=[smem(), pl.BlockSpec(memory_space=pl.ANY), vmem(), pl.BlockSpec(memory_space=pl.ANY)],
        out_specs=[vmem()] * 5,
        scratch_shapes=[
            pltpu.VMEM((384, 3072), jnp.bfloat16),
            pltpu.VMEM((512, 768), jnp.float32),
            pltpu.SemaphoreType.DMA((17,)),
        ],
        compiler_params=pltpu.CompilerParams(vmem_limit_bytes=44 * MIB),
        cost_estimate=pl.CostEstimate(
            flops=2 * 512 * 3072 * 768, bytes_accessed=8 * MIB, transcendentals=0
        ),
        name="partial_sums",
    )(info, *lines, w_own, w_sib)


def stage_kernel(info_ref, own_ref, r1_ref, r2_ref, r3_ref, o_ref, s1_ref, s2_ref, s3_ref):
    zh = info_ref[0] // 4
    for d, out in enumerate((o_ref, s1_ref, s2_ref, s3_ref)):
        i = lax.rem(zh + d, 4)
        total = own_ref[i]
        for r in (r1_ref, r2_ref, r3_ref):
            total = total + r[i].astype(jnp.float32)
        out[...] = total.astype(out.dtype)


def stage_sums(info, own, received):
    shape = (32, 768)
    return pl.pallas_call(
        stage_kernel,
        out_shape=[jax.ShapeDtypeStruct(shape, jnp.float32)]
        + [jax.ShapeDtypeStruct(shape, jnp.bfloat16)] * 3,
        in_specs=[smem()] + [vmem()] * 4,
        out_specs=[vmem()] * 4,
        compiler_params=pltpu.CompilerParams(vmem_limit_bytes=16 * MIB),
        cost_estimate=pl.CostEstimate(flops=400000, bytes_accessed=2 * MIB, transcendentals=0),
        name="stage_sums",
    )(info, own, *received)


def final_kernel(own_ref, r1_ref, r2_ref, r3_ref, o_ref, s_ref):
    total = own_ref[...]
    for r in (r1_ref, r2_ref, r3_ref):
        total = total + r[...].astype(jnp.float32)
    o_ref[...] = total[:, :384].astype(jnp.bfloat16)
    s_ref[...] = total[:, 384:].astype(jnp.bfloat16)


def final_sums(own, received):
    shape = jax.ShapeDtypeStruct((32, 384), jnp.bfloat16)
    return pl.pallas_call(
        final_kernel,
        out_shape=[shape, shape],
        in_specs=[vmem()] * 4,
        out_specs=[vmem()] * 2,
        compiler_params=pltpu.CompilerParams(vmem_limit_bytes=4 * MIB),
        cost_estimate=pl.CostEstimate(flops=100000, bytes_accessed=MIB // 4, transcendentals=0),
        name="final_sums",
    )(own, *received)


def weight_kernel(info_ref, n0_ref, n1_ref, n2_ref, n3_ref, own_ref, sib_ref, out_ref, tokens, left):

    @pl.when(pl.program_id(0) == 0)
    def _():
        z, core = info_ref[0], info_ref[3]
        for ref, far in ((n0_ref, 0), (n1_ref, -1), (n2_ref, 4 * core - 2), (n3_ref, 1)):
            for e in range(4):
                k = lax.rem(z + far + 4 * e + 16, 16)
                for which in range(2):
                    half = core if which == 0 else 1 - core
                    rows = pl.ds(pl.multiple_of(which * 512 + k * 32, 32), 32)
                    tokens[rows, :] = ref[e, pl.ds(pl.multiple_of(half * 32, 32), 32), :]
        left[...] = tokens[...].T

    total = jnp.dot(left[:, :512], own_ref[...], preferred_element_type=jnp.float32)
    total += jnp.dot(left[:, 512:], sib_ref[...], preferred_element_type=jnp.float32)
    out_ref[...] = total.astype(jnp.bfloat16)


def weight_sums(info, near, hg_own, hg_sib):
    tile = 512
    return pl.pallas_call(
        weight_kernel,
        out_shape=jax.ShapeDtypeStruct((384, 3072), jnp.bfloat16),
        grid_spec=pltpu.PrefetchScalarGridSpec(
            num_scalar_prefetch=1,
            grid=(3072 // tile,),
            in_specs=[pl.BlockSpec((4, 64, 384), lambda j, info: (0, 0, 0))] * 4
            + [pl.BlockSpec((512, tile), lambda j, info: (0, j))] * 2,
            out_specs=pl.BlockSpec((384, tile), lambda j, info: (0, j)),
            scratch_shapes=[
                pltpu.VMEM((1024, 384), jnp.bfloat16),
                pltpu.VMEM((384, 1024), jnp.bfloat16),
            ],
        ),
        compiler_params=pltpu.CompilerParams(vmem_limit_bytes=24 * MIB),
        cost_estimate=pl.CostEstimate(
            flops=2 * 1024 * 3072 * 384, bytes_accessed=10 * MIB, transcendentals=0
        ),
        name="weight_sums",
    )(info, *near, hg_own, hg_sib)


def plane_shift(first, by):
    pairs = []
    for x in range(4):
        for y in range(4):
            for core in range(2):
                along_x = (core == 0) == first
                to = ((x + by) % 4, y) if along_x else (x, (y + by) % 4)
                pairs.append(((x * 4 + y) * 2 + core, (to[0] * 4 + to[1]) * 2 + core))
    return pairs


def far_shift(by):
    return [(z, (z + 4 * by) % 16) for z in range(16)]


def column_shift(by):
    return [(z * 2 + c, (z + by[c]) % 16 * 2 + c) for z in range(16) for c in range(2)]


def second_axis_groups():
    place = [[[(x * 4 + y) * 2 + c for c in range(2)] for y in range(4)] for x in range(4)]
    along_y = [[place[j][i][0] for i in range(4)] for j in range(4)]
    along_x = [[place[i][j][1] for i in range(4)] for j in range(4)]
    return along_y + along_x


def first_axis_groups():
    place = [[[(x * 4 + y) * 2 + c for c in range(2)] for y in range(4)] for x in range(4)]
    along_x = [[place[i][j][0] for i in range(4)] for j in range(4)]
    along_y = [[place[j][i][1] for i in range(4)] for j in range(4)]
    return along_x + along_y


NEAR = ((1, 1), (2, -2), (-1, -1))


def per_device(inputs, weight, upstream, preactivation):
    core = lax.axis_index("core")
    x, y, z = lax.axis_index("x"), lax.axis_index(("yh", "yl")), lax.axis_index(Z)
    first, second = jnp.where(core == 0, x, y), jnp.where(core == 0, y, x)
    info = jnp.stack([z, first, second, core]).astype(jnp.int32)
    swap = [(0, 1), (1, 0)]

    slope = gelu_slope(preactivation.astype(jnp.float32))
    local = (upstream.astype(jnp.float32) * slope).astype(jnp.bfloat16)
    line = lax.all_gather(
        local, PLANE, axis=0, tiled=True, axis_index_groups=first_axis_groups()
    ).reshape(4, 32, 3072)
    weight_then, inputs, line = lax.optimization_barrier((weight, inputs, line))
    w_sib = lax.ppermute(weight_then, "core", swap)
    lines = lax.all_to_all(
        jnp.broadcast_to(line[None], (4, 4, 32, 3072)),
        PLANE,
        split_axis=0,
        concat_axis=0,
        tiled=True,
        axis_index_groups=second_axis_groups(),
    )
    near = [inputs] + [lax.ppermute(inputs, Z, far_shift(-d)) for d in (1, 2)]
    inputs, near[1] = lax.optimization_barrier((inputs, near[1]))
    last = lax.ppermute(inputs, Z, far_shift(-3))
    lines, near = lax.optimization_barrier((lines, near))
    lines = [lines]
    near = near + [last]

    own, *sends, hg_own = partial_sums(info, lines, weight, w_sib)
    own, near = lax.optimization_barrier((own, near))
    near, hg_own = lax.optimization_barrier((jnp.stack(near), hg_own))
    nears = [near] + [lax.ppermute(near, Z + ("core",), column_shift(by)) for by in NEAR]
    received = [
        lax.ppermute(s, Z + ("core",), column_shift(by)) for s, by in zip(sends, NEAR)
    ]
    hg_sib = lax.ppermute(hg_own, "core", swap)
    own, *sends = stage_sums(info, own, received)
    received = [
        lax.ppermute(s, Z, far_shift(d + 1))
        for d, s in enumerate(sends)
    ]
    weight_total = weight_sums(info, nears, hg_own, hg_sib)
    weight_total, *received = lax.optimization_barrier((weight_total, *received))
    mine, other = final_sums(own, received)
    other = lax.ppermute(other, "core", swap)
    input_gradient = jnp.concatenate(
        [jnp.where(core == 0, mine, other), jnp.where(core == 0, other, mine)], axis=0
    )
    return (input_gradient, weight_total)


def solution(mesh):
    fine = Mesh(
        mesh.devices.reshape(4, 2, 4, 4, 2, 2), ("x", "yh", "zh", "zl", "yl", "core")
    )
    in_specs = (P(Z, PLANE), P(PLANE, Z), P(PLANE, Z), P(PLANE, Z))
    out_specs = (P(Z, PLANE), P(PLANE, Z))
    return jax.shard_map(
        per_device, mesh=fine, in_specs=in_specs, out_specs=out_specs, check_vma=False
    )
```

```python
import math

import jax
import jax.numpy as jnp
from jax import lax
from jax.experimental import pallas as pl
from jax.experimental.pallas import tpu as pltpu
from jax.sharding import Mesh
from jax.sharding import PartitionSpec as P

gelu_scale = math.sqrt(2.0 / math.pi)
cubic_term = 0.044715

MIB = 1024 * 1024
PLANE = ("x", "yh", "yl", "core")
Z = ("zh", "zl")
ROWS_BY_ROWS = (((1,), (1,)), ((), ()))


def gelu_slope(values):
    inner = gelu_scale * (values + cubic_term * values * values * values)
    tangent = jnp.tanh(inner)
    return 0.5 * (1.0 + tangent) + 0.5 * values * (1.0 - tangent * tangent) * gelu_scale * (
        1.0 + 3.0 * cubic_term * values * values
    )


def vmem():
    return pl.BlockSpec(memory_space=pltpu.VMEM)


def smem():
    return pl.BlockSpec(memory_space=pltpu.SMEM)


def chip_number(info_ref, first, second):
    core = info_ref[3]
    return first * (4 - 3 * core) + second * (1 + 3 * core)


def block_rows(k):
    return pl.ds(pl.multiple_of(k * 32, 32), 32)


def partial_kernel(info_ref, lines_ref, w_own_ref, w_sib_ref, own_ref, send_ref, plane_ref, w, acc, sems):
    copies = []
    for j in range(4):
        for i in range(4):
            rows = block_rows(chip_number(info_ref, i, j))
            copies.append(
                pltpu.make_async_copy(lines_ref.at[j, i], plane_ref.at[rows, :], sems.at[j * 4 + i])
            )
    weights = [
        pltpu.make_async_copy(ref, w.at[n], sems.at[16 + n])
        for n, ref in enumerate((w_own_ref, w_sib_ref))
    ]
    for copy in copies + weights:
        copy.start()
    for copy in copies:
        copy.wait()
    for n, copy in enumerate(weights):
        copy.wait()
        acc[:, n * 384 : (n + 1) * 384] = lax.dot_general(
            plane_ref[...], w[n], ROWS_BY_ROWS, preferred_element_type=jnp.float32
        )
    residue = lax.rem(info_ref[0], 4)
    for x in range(4):
        own_ref[x] = acc[block_rows(x * 4 + residue), :]
        for r in range(4):
            send_ref[r, x] = acc[(x * 4 + r) * 32 : (x * 4 + r + 1) * 32, :].astype(jnp.bfloat16)


def partial_sums(info, lines, w_own, w_sib):
    return pl.pallas_call(
        partial_kernel,
        out_shape=[
            jax.ShapeDtypeStruct((4, 32, 768), jnp.float32),
            jax.ShapeDtypeStruct((4, 4, 32, 768), jnp.bfloat16),
            jax.ShapeDtypeStruct((512, 3072), jnp.bfloat16),
        ],
        in_specs=[smem()] + [pl.BlockSpec(memory_space=pl.ANY)] * 3,
        out_specs=[vmem()] * 3,
        scratch_shapes=[
            pltpu.VMEM((2, 384, 3072), jnp.bfloat16),
            pltpu.VMEM((512, 768), jnp.float32),
            pltpu.SemaphoreType.DMA((18,)),
        ],
        compiler_params=pltpu.CompilerParams(vmem_limit_bytes=44 * MIB),
        cost_estimate=pl.CostEstimate(
            flops=2 * 512 * 3072 * 768, bytes_accessed=8 * MIB, transcendentals=0
        ),
        name="partial_sums",
    )(info, *lines, w_own, w_sib)


def stage_kernel(info_ref, own_ref, r_ref, out_ref):
    residue, core = lax.rem(info_ref[0], 4), info_ref[3]
    for i in range(4):
        total = own_ref[i]
        for d in range(1, 4):
            total = total + r_ref[lax.rem(residue + d, 4), i].astype(jnp.float32)
        total = total.astype(jnp.bfloat16)
        out_ref[i, core] = total[:, :384]
        out_ref[i, 1 - core] = total[:, 384:]


def stage_sums(info, own, received):
    return pl.pallas_call(
        stage_kernel,
        out_shape=jax.ShapeDtypeStruct((4, 2, 32, 384), jnp.bfloat16),
        in_specs=[smem()] + [vmem()] * 2,
        out_specs=vmem(),
        compiler_params=pltpu.CompilerParams(vmem_limit_bytes=8 * MIB),
        cost_estimate=pl.CostEstimate(flops=400000, bytes_accessed=MIB, transcendentals=0),
        name="stage_sums",
    )(info, own, received)


def weight_kernel(info_ref, n0_ref, n1_ref, n2_ref, n3_ref, own_ref, sib_ref, out_ref, tokens, left):

    @pl.when(pl.program_id(0) == 0)
    def _():
        z, core = info_ref[0], info_ref[3]
        for ref, far in ((n0_ref, 0), (n1_ref, -1), (n2_ref, 4 * core - 2), (n3_ref, 1)):
            for e in range(4):
                k = lax.rem(z + far + 4 * e + 16, 16)
                for which in range(2):
                    half = core if which == 0 else 1 - core
                    rows = pl.ds(pl.multiple_of(which * 512 + k * 32, 32), 32)
                    tokens[rows, :] = ref[e, pl.ds(pl.multiple_of(half * 32, 32), 32), :]
        left[...] = tokens[...].T

    total = jnp.dot(left[:, :512], own_ref[...], preferred_element_type=jnp.float32)
    total += jnp.dot(left[:, 512:], sib_ref[...], preferred_element_type=jnp.float32)
    out_ref[...] = total.astype(jnp.bfloat16)


def weight_sums(info, near, hg_own, hg_sib):
    tile = 512
    return pl.pallas_call(
        weight_kernel,
        out_shape=jax.ShapeDtypeStruct((384, 3072), jnp.bfloat16),
        grid_spec=pltpu.PrefetchScalarGridSpec(
            num_scalar_prefetch=1,
            grid=(3072 // tile,),
            in_specs=[pl.BlockSpec((4, 64, 384), lambda j, info: (0, 0, 0))] * 4
            + [pl.BlockSpec((512, tile), lambda j, info: (0, j))] * 2,
            out_specs=pl.BlockSpec((384, tile), lambda j, info: (0, j)),
            scratch_shapes=[
                pltpu.VMEM((1024, 384), jnp.bfloat16),
                pltpu.VMEM((384, 1024), jnp.bfloat16),
            ],
        ),
        compiler_params=pltpu.CompilerParams(vmem_limit_bytes=24 * MIB),
        cost_estimate=pl.CostEstimate(
            flops=2 * 1024 * 3072 * 384, bytes_accessed=10 * MIB, transcendentals=0
        ),
        name="weight_sums",
    )(info, *near, hg_own, hg_sib)


def plane_shift(first, by):
    pairs = []
    for x in range(4):
        for y in range(4):
            for core in range(2):
                along_x = (core == 0) == first
                to = ((x + by) % 4, y) if along_x else (x, (y + by) % 4)
                pairs.append(((x * 4 + y) * 2 + core, (to[0] * 4 + to[1]) * 2 + core))
    return pairs


def near_groups():
    groups = []
    for start in range(0, 16, 4):
        groups.append([(start + i) * 2 for i in range(4)])
        groups.append([(start + i) % 16 * 2 + 1 for i in (4, 5, 2, 3)])
    return groups


def far_shift(by):
    return [(z, (z + 4 * by) % 16) for z in range(16)]


def column_shift(by):
    return [(z * 2 + c, (z + by[c]) % 16 * 2 + c) for z in range(16) for c in range(2)]


def second_axis_groups():
    place = [[[(x * 4 + y) * 2 + c for c in range(2)] for y in range(4)] for x in range(4)]
    along_y = [[place[j][i][0] for i in range(4)] for j in range(4)]
    along_x = [[place[i][j][1] for i in range(4)] for j in range(4)]
    return along_y + along_x


def first_axis_groups():
    place = [[[(x * 4 + y) * 2 + c for c in range(2)] for y in range(4)] for x in range(4)]
    along_x = [[place[i][j][0] for i in range(4)] for j in range(4)]
    along_y = [[place[j][i][1] for i in range(4)] for j in range(4)]
    return along_x + along_y


NEAR = ((1, 1), (2, -2), (-1, -1))


def per_device(inputs, weight, upstream, preactivation):
    core = lax.axis_index("core")
    x, y, z = lax.axis_index("x"), lax.axis_index(("yh", "yl")), lax.axis_index(Z)
    first, second = jnp.where(core == 0, x, y), jnp.where(core == 0, y, x)
    info = jnp.stack([z, first, second, core]).astype(jnp.int32)
    swap = [(0, 1), (1, 0)]

    slope = gelu_slope(preactivation.astype(jnp.float32))
    local = (upstream.astype(jnp.float32) * slope).astype(jnp.bfloat16)
    line = lax.all_gather(
        local, PLANE, axis=0, tiled=True, axis_index_groups=first_axis_groups()
    ).reshape(4, 32, 3072)
    weight_then, inputs, line = lax.optimization_barrier((weight, inputs, line))
    w_sib = lax.ppermute(weight_then, "core", swap)
    lines = lax.all_to_all(
        jnp.broadcast_to(line[None], (4, 4, 32, 3072)),
        PLANE,
        split_axis=0,
        concat_axis=0,
        tiled=True,
        axis_index_groups=second_axis_groups(),
    )
    near = [inputs] + [lax.ppermute(inputs, Z, far_shift(-d)) for d in (1, 2, 3)]

    own, send, hg_own = partial_sums(info, [lines], weight, w_sib)
    received = lax.all_to_all(
        send,
        Z + ("core",),
        split_axis=0,
        concat_axis=0,
        tiled=True,
        axis_index_groups=near_groups(),
    )
    own, near = lax.optimization_barrier((own, near))
    near, hg_own = lax.optimization_barrier((jnp.stack(near), hg_own))
    nears = [near] + [lax.ppermute(near, Z + ("core",), column_shift(by)) for by in NEAR]
    hg_sib = lax.ppermute(hg_own, "core", swap)
    summed = stage_sums(info, own, received).reshape(8, 32, 384)
    summed, nears = lax.optimization_barrier((summed, nears))
    summed = lax.all_to_all(summed, ("zh", "core"), split_axis=0, concat_axis=0, tiled=True)
    weight_total = weight_sums(info, nears, hg_own, hg_sib)
    weight_total, summed = lax.optimization_barrier((weight_total, summed))
    summed = summed.reshape(4, 64, 384).astype(jnp.float32)
    input_gradient = (summed[0] + summed[1] + summed[2] + summed[3]).astype(jnp.bfloat16)
    return (input_gradient, weight_total)


def solution(mesh):
    fine = Mesh(
        mesh.devices.reshape(4, 2, 4, 4, 2, 2), ("x", "yh", "zh", "zl", "yl", "core")
    )
    in_specs = (P(Z, PLANE), P(PLANE, Z), P(PLANE, Z), P(PLANE, Z))
    out_specs = (P(Z, PLANE), P(PLANE, Z))
    return jax.shard_map(
        per_device, mesh=fine, in_specs=in_specs, out_specs=out_specs, check_vma=False
    )
```

```python
import math

import jax
import jax.numpy as jnp
from jax import lax
from jax.experimental import pallas as pl
from jax.experimental.pallas import tpu as pltpu
from jax.sharding import Mesh
from jax.sharding import PartitionSpec as P

gelu_scale = math.sqrt(2.0 / math.pi)
cubic_term = 0.044715

MIB = 1024 * 1024
PLANE = ("x", "yh", "yl", "core")
Z = ("zh", "zl")
ROWS_BY_ROWS = (((1,), (1,)), ((), ()))


def gelu_slope(values):
    inner = gelu_scale * (values + cubic_term * values * values * values)
    tangent = jnp.tanh(inner)
    return 0.5 * (1.0 + tangent) + 0.5 * values * (1.0 - tangent * tangent) * gelu_scale * (
        1.0 + 3.0 * cubic_term * values * values
    )


def vmem():
    return pl.BlockSpec(memory_space=pltpu.VMEM)


def smem():
    return pl.BlockSpec(memory_space=pltpu.SMEM)


def block_rows(k):
    return pl.ds(pl.multiple_of(k * 32, 32), 32)


def partial_kernel(info_ref, plane_ref, w_own_ref, w_sib_ref, own_ref, s1_ref, s2_ref, s3_ref, acc):
    for n, w_ref in enumerate((w_own_ref, w_sib_ref)):
        acc[:, n * 384 : (n + 1) * 384] = lax.dot_general(
            plane_ref[...], w_ref[...], ROWS_BY_ROWS, preferred_element_type=jnp.float32
        )
    for d, out in enumerate((own_ref, s1_ref, s2_ref, s3_ref)):
        residue = lax.rem(info_ref[0] + d, 4)
        for x in range(4):
            out[x] = acc[block_rows(x * 4 + residue), :].astype(out.dtype)


def partial_sums(info, plane, w_own, w_sib):
    shape = (4, 32, 768)
    return pl.pallas_call(
        partial_kernel,
        out_shape=[jax.ShapeDtypeStruct(shape, jnp.float32)]
        + [jax.ShapeDtypeStruct(shape, jnp.bfloat16)] * 3,
        in_specs=[smem()] + [vmem()] * 3,
        out_specs=[vmem()] * 4,
        scratch_shapes=[pltpu.VMEM((512, 768), jnp.float32)],
        compiler_params=pltpu.CompilerParams(vmem_limit_bytes=20 * MIB),
        cost_estimate=pl.CostEstimate(
            flops=2 * 512 * 3072 * 768, bytes_accessed=8 * MIB, transcendentals=0
        ),
        name="partial_sums",
    )(info, plane, w_own, w_sib)


def stage_kernel(info_ref, own_ref, r1_ref, r2_ref, r3_ref, o_ref, s1_ref, s2_ref, s3_ref):
    zh = info_ref[0] // 4
    for d, out in enumerate((o_ref, s1_ref, s2_ref, s3_ref)):
        i = lax.rem(zh + d, 4)
        total = own_ref[i]
        for r in (r1_ref, r2_ref, r3_ref):
            total = total + r[i].astype(jnp.float32)
        out[...] = total.astype(out.dtype)


def stage_sums(info, own, received):
    shape = (32, 768)
    return pl.pallas_call(
        stage_kernel,
        out_shape=[jax.ShapeDtypeStruct(shape, jnp.float32)]
        + [jax.ShapeDtypeStruct(shape, jnp.bfloat16)] * 3,
        in_specs=[smem()] + [vmem()] * 4,
        out_specs=[vmem()] * 4,
        compiler_params=pltpu.CompilerParams(vmem_limit_bytes=16 * MIB),
        cost_estimate=pl.CostEstimate(flops=400000, bytes_accessed=2 * MIB, transcendentals=0),
        name="stage_sums",
    )(info, own, *received)


def final_kernel(own_ref, r1_ref, r2_ref, r3_ref, o_ref, s_ref):
    total = own_ref[...]
    for r in (r1_ref, r2_ref, r3_ref):
        total = total + r[...].astype(jnp.float32)
    o_ref[...] = total[:, :384].astype(jnp.bfloat16)
    s_ref[...] = total[:, 384:].astype(jnp.bfloat16)


def final_sums(own, received):
    shape = jax.ShapeDtypeStruct((32, 384), jnp.bfloat16)
    return pl.pallas_call(
        final_kernel,
        out_shape=[shape, shape],
        in_specs=[vmem()] * 4,
        out_specs=[vmem()] * 2,
        compiler_params=pltpu.CompilerParams(vmem_limit_bytes=4 * MIB),
        cost_estimate=pl.CostEstimate(flops=100000, bytes_accessed=MIB // 4, transcendentals=0),
        name="final_sums",
    )(own, *received)


def weight_kernel(info_ref, n0_ref, n1_ref, n2_ref, n3_ref, own_ref, sib_ref, out_ref, tokens, left):

    @pl.when(pl.program_id(0) == 0)
    def _():
        z, core = info_ref[0], info_ref[1]
        for ref, far in ((n0_ref, 0), (n1_ref, -1), (n2_ref, 4 * core - 2), (n3_ref, 1)):
            for e in range(4):
                k = lax.rem(z + far + 4 * e + 16, 16)
                for which in range(2):
                    half = core if which == 0 else 1 - core
                    rows = pl.ds(pl.multiple_of(which * 512 + k * 32, 32), 32)
                    tokens[rows, :] = ref[e, pl.ds(pl.multiple_of(half * 32, 32), 32), :]
        left[...] = tokens[...].T

    total = jnp.dot(left[:, :512], own_ref[...], preferred_element_type=jnp.float32)
    total += jnp.dot(left[:, 512:], sib_ref[...], preferred_element_type=jnp.float32)
    out_ref[...] = total.astype(jnp.bfloat16)


def weight_sums(info, near, hg_own, hg_sib):
    tile = 512
    return pl.pallas_call(
        weight_kernel,
        out_shape=jax.ShapeDtypeStruct((384, 3072), jnp.bfloat16),
        grid_spec=pltpu.PrefetchScalarGridSpec(
            num_scalar_prefetch=1,
            grid=(3072 // tile,),
            in_specs=[pl.BlockSpec((4, 64, 384), lambda j, info: (0, 0, 0))] * 4
            + [pl.BlockSpec((512, tile), lambda j, info: (0, j))] * 2,
            out_specs=pl.BlockSpec((384, tile), lambda j, info: (0, j)),
            scratch_shapes=[
                pltpu.VMEM((1024, 384), jnp.bfloat16),
                pltpu.VMEM((384, 1024), jnp.bfloat16),
            ],
        ),
        compiler_params=pltpu.CompilerParams(vmem_limit_bytes=24 * MIB),
        cost_estimate=pl.CostEstimate(
            flops=2 * 1024 * 3072 * 384, bytes_accessed=10 * MIB, transcendentals=0
        ),
        name="weight_sums",
    )(info, *near, hg_own, hg_sib)


def far_shift(by):
    return [(z, (z + 4 * by) % 16) for z in range(16)]


def column_shift(by):
    return [(z * 2 + c, (z + by[c]) % 16 * 2 + c) for z in range(16) for c in range(2)]


NEAR = ((1, 1), (2, -2), (-1, -1))


def per_device(inputs, weight, upstream, preactivation):
    core = lax.axis_index("core")
    info = jnp.stack([lax.axis_index(Z), core]).astype(jnp.int32)
    swap = [(0, 1), (1, 0)]

    slope = gelu_slope(preactivation.astype(jnp.float32))
    local = (upstream.astype(jnp.float32) * slope).astype(jnp.bfloat16)
    hg_own = lax.all_to_all(
        jnp.broadcast_to(local[None], (16, 32, 3072)),
        ("x", "yh", "yl"),
        split_axis=0,
        concat_axis=0,
        tiled=True,
    ).reshape(512, 3072)
    weight_then, inputs, local = lax.optimization_barrier((weight, inputs, local))
    w_sib = lax.ppermute(weight_then, "core", swap)
    near = [inputs] + [lax.ppermute(inputs, Z, far_shift(-d)) for d in (1, 2, 3)]
    near, w_sib = lax.optimization_barrier((near, w_sib))
    near = jnp.stack(near)
    nears = [near] + [lax.ppermute(near, Z + ("core",), column_shift(by)) for by in NEAR]
    hg_own, nears = lax.optimization_barrier((hg_own, nears))

    own, *sends = partial_sums(info, hg_own, weight, w_sib)
    received = [
        lax.ppermute(s, Z + ("core",), column_shift(by)) for s, by in zip(sends, NEAR)
    ]
    hg_sib = lax.ppermute(hg_own, "core", swap)
    own, *sends = stage_sums(info, own, received)
    received = [
        lax.ppermute(s, Z, far_shift(d + 1))
        for d, s in enumerate(sends)
    ]
    weight_total = weight_sums(info, nears, hg_own, hg_sib)
    weight_total, *received = lax.optimization_barrier((weight_total, *received))
    mine, other = final_sums(own, received)
    other = lax.ppermute(other, "core", swap)
    input_gradient = jnp.concatenate(
        [jnp.where(core == 0, mine, other), jnp.where(core == 0, other, mine)], axis=0
    )
    return (input_gradient, weight_total)


def solution(mesh):
    fine = Mesh(
        mesh.devices.reshape(4, 2, 4, 4, 2, 2), ("x", "yh", "zh", "zl", "yl", "core")
    )
    in_specs = (P(Z, PLANE), P(PLANE, Z), P(PLANE, Z), P(PLANE, Z))
    out_specs = (P(Z, PLANE), P(PLANE, Z))
    return jax.shard_map(
        per_device, mesh=fine, in_specs=in_specs, out_specs=out_specs, check_vma=False
    )
```

```python
import math

import jax
import jax.numpy as jnp
from jax import lax
from jax.experimental import pallas as pl
from jax.experimental.pallas import tpu as pltpu
from jax.sharding import Mesh
from jax.sharding import PartitionSpec as P

gelu_scale = math.sqrt(2.0 / math.pi)
cubic_term = 0.044715

MIB = 1024 * 1024
PLANE = ("x", "yh", "yl", "core")
Z = ("zh", "zl")
ROWS_BY_ROWS = (((1,), (1,)), ((), ()))


def gelu_slope(values):
    inner = gelu_scale * (values + cubic_term * values * values * values)
    tangent = jnp.tanh(inner)
    return 0.5 * (1.0 + tangent) + 0.5 * values * (1.0 - tangent * tangent) * gelu_scale * (
        1.0 + 3.0 * cubic_term * values * values
    )


def vmem():
    return pl.BlockSpec(memory_space=pltpu.VMEM)


def smem():
    return pl.BlockSpec(memory_space=pltpu.SMEM)


def chip_number(info_ref, first, second):
    core = info_ref[3]
    return first * (4 - 3 * core) + second * (1 + 3 * core)


def block_rows(k):
    return pl.ds(pl.multiple_of(k * 32, 32), 32)


def partial_kernel(info_ref, lines_ref, w_own_ref, w_sib_ref, own_ref, send_ref, plane_ref, w_sib, acc, sems):
    copies = []
    for j in range(4):
        for i in range(4):
            rows = block_rows(chip_number(info_ref, i, j))
            copies.append(
                pltpu.make_async_copy(lines_ref.at[j, i], plane_ref.at[rows, :], sems.at[j * 4 + i])
            )
    weights = pltpu.make_async_copy(w_sib_ref, w_sib, sems.at[16])
    for copy in copies:
        copy.start()
    weights.start()
    for copy in copies:
        copy.wait()
    acc[:, :384] = lax.dot_general(
        plane_ref[...], w_own_ref[...], ROWS_BY_ROWS, preferred_element_type=jnp.float32
    )
    weights.wait()
    acc[:, 384:] = lax.dot_general(
        plane_ref[...], w_sib[...], ROWS_BY_ROWS, preferred_element_type=jnp.float32
    )
    z, by = info_ref[0], 1 + 2 * info_ref[3]
    for j in range(2):
        for x in range(4):
            k = x * 4 + lax.rem(z + 2 * j, 4)
            own_ref[j, x] = acc[block_rows(k), :]
            k = x * 4 + lax.rem(z + by + 2 * j, 4)
            send_ref[j, x] = acc[block_rows(k), :].astype(jnp.bfloat16)


def partial_sums(info, lines, w_own, w_sib):
    shape = (2, 4, 32, 768)
    return pl.pallas_call(
        partial_kernel,
        out_shape=[
            jax.ShapeDtypeStruct(shape, jnp.float32),
            jax.ShapeDtypeStruct(shape, jnp.bfloat16),
            jax.ShapeDtypeStruct((512, 3072), jnp.bfloat16),
        ],
        in_specs=[smem(), pl.BlockSpec(memory_space=pl.ANY), vmem(), pl.BlockSpec(memory_space=pl.ANY)],
        out_specs=[vmem()] * 3,
        scratch_shapes=[
            pltpu.VMEM((384, 3072), jnp.bfloat16),
            pltpu.VMEM((512, 768), jnp.float32),
            pltpu.SemaphoreType.DMA((17,)),
        ],
        compiler_params=pltpu.CompilerParams(vmem_limit_bytes=44 * MIB),
        cost_estimate=pl.CostEstimate(
            flops=2 * 512 * 3072 * 768, bytes_accessed=8 * MIB, transcendentals=0
        ),
        name="partial_sums",
    )(info, *lines, w_own, w_sib)


def pair_kernel(own_ref, r_ref, keep_ref, send_ref):
    keep_ref[...] = own_ref[0] + r_ref[0].astype(jnp.float32)
    send_ref[...] = (own_ref[1] + r_ref[1].astype(jnp.float32)).astype(jnp.bfloat16)


def pair_sums(own, received):
    shape = (4, 32, 768)
    return pl.pallas_call(
        pair_kernel,
        out_shape=[
            jax.ShapeDtypeStruct(shape, jnp.float32),
            jax.ShapeDtypeStruct(shape, jnp.bfloat16),
        ],
        in_specs=[vmem()] * 2,
        out_specs=[vmem()] * 2,
        compiler_params=pltpu.CompilerParams(vmem_limit_bytes=8 * MIB),
        cost_estimate=pl.CostEstimate(flops=400000, bytes_accessed=2 * MIB, transcendentals=0),
        name="pair_sums",
    )(own, received)


def stage_kernel(info_ref, own_ref, r_ref, o_ref, s1_ref, s2_ref, s3_ref):
    zh = info_ref[0] // 4
    for d, out in enumerate((o_ref, s1_ref, s2_ref, s3_ref)):
        i = lax.rem(zh + d, 4)
        out[...] = (own_ref[i] + r_ref[i].astype(jnp.float32)).astype(out.dtype)


def stage_sums(info, own, received):
    shape = (32, 768)
    return pl.pallas_call(
        stage_kernel,
        out_shape=[jax.ShapeDtypeStruct(shape, jnp.float32)]
        + [jax.ShapeDtypeStruct(shape, jnp.bfloat16)] * 3,
        in_specs=[smem()] + [vmem()] * 2,
        out_specs=[vmem()] * 4,
        compiler_params=pltpu.CompilerParams(vmem_limit_bytes=8 * MIB),
        cost_estimate=pl.CostEstimate(flops=400000, bytes_accessed=MIB, transcendentals=0),
        name="stage_sums",
    )(info, own, received)


def final_kernel(own_ref, r1_ref, r2_ref, r3_ref, o_ref, s_ref):
    total = own_ref[...]
    for r in (r1_ref, r2_ref, r3_ref):
        total = total + r[...].astype(jnp.float32)
    o_ref[...] = total[:, :384].astype(jnp.bfloat16)
    s_ref[...] = total[:, 384:].astype(jnp.bfloat16)


def final_sums(own, received):
    shape = jax.ShapeDtypeStruct((32, 384), jnp.bfloat16)
    return pl.pallas_call(
        final_kernel,
        out_shape=[shape, shape],
        in_specs=[vmem()] * 4,
        out_specs=[vmem()] * 2,
        compiler_params=pltpu.CompilerParams(vmem_limit_bytes=4 * MIB),
        cost_estimate=pl.CostEstimate(flops=100000, bytes_accessed=MIB // 4, transcendentals=0),
        name="final_sums",
    )(own, *received)


def weight_kernel(info_ref, n0_ref, n1_ref, n2_ref, n3_ref, own_ref, sib_ref, out_ref, tokens, left):

    @pl.when(pl.program_id(0) == 0)
    def _():
        z, core = info_ref[0], info_ref[3]
        for ref, far in (
            (n0_ref, 0),
            (n1_ref, 1 - 2 * core),
            (n2_ref, 2 - 4 * core),
            (n3_ref, 2 * core - 1),
        ):
            for e in range(4):
                k = lax.rem(z + far + 4 * e + 16, 16)
                for which in range(2):
                    half = core if which == 0 else 1 - core
                    rows = pl.ds(pl.multiple_of(which * 512 + k * 32, 32), 32)
                    tokens[rows, :] = ref[e, pl.ds(pl.multiple_of(half * 32, 32), 32), :]
        left[...] = tokens[...].T

    total = jnp.dot(left[:, :512], own_ref[...], preferred_element_type=jnp.float32)
    total += jnp.dot(left[:, 512:], sib_ref[...], preferred_element_type=jnp.float32)
    out_ref[...] = total.astype(jnp.bfloat16)


def weight_sums(info, near, hg_own, hg_sib):
    tile = 512
    return pl.pallas_call(
        weight_kernel,
        out_shape=jax.ShapeDtypeStruct((384, 3072), jnp.bfloat16),
        grid_spec=pltpu.PrefetchScalarGridSpec(
            num_scalar_prefetch=1,
            grid=(3072 // tile,),
            in_specs=[pl.BlockSpec((4, 64, 384), lambda j, info: (0, 0, 0))] * 4
            + [pl.BlockSpec((512, tile), lambda j, info: (0, j))] * 2,
            out_specs=pl.BlockSpec((384, tile), lambda j, info: (0, j)),
            scratch_shapes=[
                pltpu.VMEM((1024, 384), jnp.bfloat16),
                pltpu.VMEM((384, 1024), jnp.bfloat16),
            ],
        ),
        compiler_params=pltpu.CompilerParams(vmem_limit_bytes=24 * MIB),
        cost_estimate=pl.CostEstimate(
            flops=2 * 1024 * 3072 * 384, bytes_accessed=10 * MIB, transcendentals=0
        ),
        name="weight_sums",
    )(info, *near, hg_own, hg_sib)


def plane_shift(first, by):
    pairs = []
    for x in range(4):
        for y in range(4):
            for core in range(2):
                along_x = (core == 0) == first
                to = ((x + by) % 4, y) if along_x else (x, (y + by) % 4)
                pairs.append(((x * 4 + y) * 2 + core, (to[0] * 4 + to[1]) * 2 + core))
    return pairs


def far_shift(by):
    return [(z, (z + 4 * by) % 16) for z in range(16)]


def column_shift(by):
    return [(z * 2 + c, (z + by[c]) % 16 * 2 + c) for z in range(16) for c in range(2)]


def second_axis_groups():
    place = [[[(x * 4 + y) * 2 + c for c in range(2)] for y in range(4)] for x in range(4)]
    along_y = [[place[j][i][0] for i in range(4)] for j in range(4)]
    along_x = [[place[i][j][1] for i in range(4)] for j in range(4)]
    return along_y + along_x


def first_axis_groups():
    place = [[[(x * 4 + y) * 2 + c for c in range(2)] for y in range(4)] for x in range(4)]
    along_x = [[place[i][j][0] for i in range(4)] for j in range(4)]
    along_y = [[place[j][i][1] for i in range(4)] for j in range(4)]
    return along_x + along_y


NEAR = ((-1, 1), (-2, 2), (1, -1))


def per_device(inputs, weight, upstream, preactivation):
    core = lax.axis_index("core")
    x, y, z = lax.axis_index("x"), lax.axis_index(("yh", "yl")), lax.axis_index(Z)
    first, second = jnp.where(core == 0, x, y), jnp.where(core == 0, y, x)
    info = jnp.stack([z, first, second, core]).astype(jnp.int32)
    swap = [(0, 1), (1, 0)]

    slope = gelu_slope(preactivation.astype(jnp.float32))
    local = (upstream.astype(jnp.float32) * slope).astype(jnp.bfloat16)
    line = lax.all_gather(
        local, PLANE, axis=0, tiled=True, axis_index_groups=first_axis_groups()
    ).reshape(4, 32, 3072)
    weight_then, inputs, line = lax.optimization_barrier((weight, inputs, line))
    w_sib = lax.ppermute(weight_then, "core", swap)
    lines = lax.all_to_all(
        jnp.broadcast_to(line[None], (4, 4, 32, 3072)),
        PLANE,
        split_axis=0,
        concat_axis=0,
        tiled=True,
        axis_index_groups=second_axis_groups(),
    )
    near = [inputs] + [lax.ppermute(inputs, Z, far_shift(-d)) for d in (1, 2)]
    inputs, near[1] = lax.optimization_barrier((inputs, near[1]))
    last = lax.ppermute(inputs, Z, far_shift(-3))
    lines, near = lax.optimization_barrier((lines, near))
    lines = [lines]
    near = near + [last]

    own, send, hg_own = partial_sums(info, lines, weight, w_sib)
    own, near = lax.optimization_barrier((own, near))
    near, hg_own = lax.optimization_barrier((jnp.stack(near), hg_own))
    nears = [near] + [lax.ppermute(near, Z + ("core",), column_shift(by)) for by in NEAR]
    received = lax.ppermute(send, Z + ("core",), column_shift((1, -1)))
    received, nears[1] = lax.optimization_barrier((received, nears[1]))
    own, send = pair_sums(own, received)
    received = lax.ppermute(send, Z + ("core",), column_shift((2, -2)))
    hg_sib = lax.ppermute(hg_own, "core", swap)
    own, *sends = stage_sums(info, own, received)
    received = [
        lax.ppermute(s, Z, far_shift(d + 1))
        for d, s in enumerate(sends)
    ]
    weight_total = weight_sums(info, nears, hg_own, hg_sib)
    weight_total, *received = lax.optimization_barrier((weight_total, *received))
    mine, other = final_sums(own, received)
    other = lax.ppermute(other, "core", swap)
    input_gradient = jnp.concatenate(
        [jnp.where(core == 0, mine, other), jnp.where(core == 0, other, mine)], axis=0
    )
    return (input_gradient, weight_total)


def solution(mesh):
    fine = Mesh(
        mesh.devices.reshape(4, 2, 4, 4, 2, 2), ("x", "yh", "zh", "zl", "yl", "core")
    )
    in_specs = (P(Z, PLANE), P(PLANE, Z), P(PLANE, Z), P(PLANE, Z))
    out_specs = (P(Z, PLANE), P(PLANE, Z))
    return jax.shard_map(
        per_device, mesh=fine, in_specs=in_specs, out_specs=out_specs, check_vma=False
    )
```

```python
import math

import jax
import jax.numpy as jnp
from jax import lax
from jax.experimental import pallas as pl
from jax.experimental.pallas import tpu as pltpu
from jax.sharding import Mesh
from jax.sharding import PartitionSpec as P

gelu_scale = math.sqrt(2.0 / math.pi)
cubic_term = 0.044715

MIB = 1024 * 1024
PLANE = ("x", "yh", "yl", "core")
Z = ("zh", "zl")
ROWS_BY_ROWS = (((1,), (1,)), ((), ()))


def gelu_slope(values):
    inner = gelu_scale * (values + cubic_term * values * values * values)
    tangent = jnp.tanh(inner)
    return 0.5 * (1.0 + tangent) + 0.5 * values * (1.0 - tangent * tangent) * gelu_scale * (
        1.0 + 3.0 * cubic_term * values * values
    )


def vmem():
    return pl.BlockSpec(memory_space=pltpu.VMEM)


def smem():
    return pl.BlockSpec(memory_space=pltpu.SMEM)


def block_rows(k):
    return pl.ds(pl.multiple_of(k * 32, 32), 32)


def place(core, x, y):
    return x * (1 + 3 * core) + y * (4 - 3 * core)


def own_kernel(lines_ref, w_ref, out_ref):
    out_ref[...] = lax.dot_general(
        lines_ref[...], w_ref[...], ROWS_BY_ROWS, preferred_element_type=jnp.float32
    )


def own_sums(lines, w):
    return pl.pallas_call(
        own_kernel,
        out_shape=jax.ShapeDtypeStruct((512, 384), jnp.float32),
        in_specs=[vmem()] * 2,
        out_specs=vmem(),
        compiler_params=pltpu.CompilerParams(vmem_limit_bytes=16 * MIB),
        cost_estimate=pl.CostEstimate(
            flops=2 * 512 * 3072 * 384, bytes_accessed=6 * MIB, transcendentals=0
        ),
        name="own_sums",
    )(lines, w)


def sib_kernel(info_ref, sums_ref, lines_ref, w_ref, own_ref, s1_ref, s2_ref, s3_ref, acc):
    acc[...] = lax.dot_general(
        lines_ref[...], w_ref[...], ROWS_BY_ROWS, preferred_element_type=jnp.float32
    )
    core = info_ref[1]
    for d, out in enumerate((own_ref, s1_ref, s2_ref, s3_ref)):
        residue = lax.rem(info_ref[0] + d, 4)
        for x in range(4):
            mine = sums_ref[block_rows(place(core, x, residue)), :]
            theirs = acc[block_rows(place(1 - core, x, residue)), :]
            out[x, block_rows(core), :] = mine.astype(out.dtype)
            out[x, block_rows(1 - core), :] = theirs.astype(out.dtype)


def sib_sums(info, sums, lines, w):
    shape = (4, 64, 384)
    return pl.pallas_call(
        sib_kernel,
        out_shape=[jax.ShapeDtypeStruct(shape, jnp.float32)]
        + [jax.ShapeDtypeStruct(shape, jnp.bfloat16)] * 3,
        in_specs=[smem()] + [vmem()] * 3,
        out_specs=[vmem()] * 4,
        scratch_shapes=[pltpu.VMEM((512, 384), jnp.float32)],
        compiler_params=pltpu.CompilerParams(vmem_limit_bytes=16 * MIB),
        cost_estimate=pl.CostEstimate(
            flops=2 * 512 * 3072 * 384, bytes_accessed=8 * MIB, transcendentals=0
        ),
        name="sib_sums",
    )(info, sums, lines, w)


def stage_kernel(info_ref, own_ref, r1_ref, r2_ref, r3_ref, o_ref, s1_ref, s2_ref, s3_ref):
    zh = info_ref[0] // 4
    for d, out in enumerate((o_ref, s1_ref, s2_ref, s3_ref)):
        i = lax.rem(zh + d, 4)
        total = own_ref[i]
        for r in (r1_ref, r2_ref, r3_ref):
            total = total + r[i].astype(jnp.float32)
        out[...] = total.astype(out.dtype)


def stage_sums(info, own, received):
    shape = (64, 384)
    return pl.pallas_call(
        stage_kernel,
        out_shape=[jax.ShapeDtypeStruct(shape, jnp.float32)]
        + [jax.ShapeDtypeStruct(shape, jnp.bfloat16)] * 3,
        in_specs=[smem()] + [vmem()] * 4,
        out_specs=[vmem()] * 4,
        compiler_params=pltpu.CompilerParams(vmem_limit_bytes=16 * MIB),
        cost_estimate=pl.CostEstimate(flops=400000, bytes_accessed=2 * MIB, transcendentals=0),
        name="stage_sums",
    )(info, own, *received)


def final_kernel(own_ref, r1_ref, r2_ref, r3_ref, out_ref):
    total = own_ref[...]
    for r in (r1_ref, r2_ref, r3_ref):
        total = total + r[...].astype(jnp.float32)
    out_ref[...] = total.astype(jnp.bfloat16)


def final_sums(own, received):
    return pl.pallas_call(
        final_kernel,
        out_shape=jax.ShapeDtypeStruct((64, 384), jnp.bfloat16),
        in_specs=[vmem()] * 4,
        out_specs=vmem(),
        compiler_params=pltpu.CompilerParams(vmem_limit_bytes=4 * MIB),
        cost_estimate=pl.CostEstimate(flops=100000, bytes_accessed=MIB // 4, transcendentals=0),
        name="final_sums",
    )(own, *received)


def weight_kernel(info_ref, n0_ref, n1_ref, n2_ref, n3_ref, own_ref, sib_ref, out_ref, tokens, left):

    @pl.when(pl.program_id(0) == 0)
    def _():
        z, core = info_ref[0], info_ref[1]
        for ref, far in ((n0_ref, 0), (n1_ref, -1), (n2_ref, 4 * core - 2), (n3_ref, 1)):
            for e in range(4):
                k = lax.rem(z + far + 4 * e + 16, 16)
                for which in range(2):
                    half = core if which == 0 else 1 - core
                    at = place(half, k // 4, lax.rem(k, 4))
                    rows = pl.ds(pl.multiple_of(which * 512 + at * 32, 32), 32)
                    tokens[rows, :] = ref[e, pl.ds(pl.multiple_of(half * 32, 32), 32), :]
        left[...] = tokens[...].T

    total = jnp.dot(left[:, :512], own_ref[...], preferred_element_type=jnp.float32)
    total += jnp.dot(left[:, 512:], sib_ref[...], preferred_element_type=jnp.float32)
    out_ref[...] = total.astype(jnp.bfloat16)


def weight_sums(info, near, hg_own, hg_sib):
    tile = 512
    return pl.pallas_call(
        weight_kernel,
        out_shape=jax.ShapeDtypeStruct((384, 3072), jnp.bfloat16),
        grid_spec=pltpu.PrefetchScalarGridSpec(
            num_scalar_prefetch=1,
            grid=(3072 // tile,),
            in_specs=[pl.BlockSpec((4, 64, 384), lambda j, info: (0, 0, 0))] * 4
            + [pl.BlockSpec((512, tile), lambda j, info: (0, j))] * 2,
            out_specs=pl.BlockSpec((384, tile), lambda j, info: (0, j)),
            scratch_shapes=[
                pltpu.VMEM((1024, 384), jnp.bfloat16),
                pltpu.VMEM((384, 1024), jnp.bfloat16),
            ],
        ),
        compiler_params=pltpu.CompilerParams(vmem_limit_bytes=24 * MIB),
        cost_estimate=pl.CostEstimate(
            flops=2 * 1024 * 3072 * 384, bytes_accessed=10 * MIB, transcendentals=0
        ),
        name="weight_sums",
    )(info, *near, hg_own, hg_sib)


def plane_shift(first, by):
    pairs = []
    for x in range(4):
        for y in range(4):
            for core in range(2):
                along_x = (core == 0) == first
                to = ((x + by) % 4, y) if along_x else (x, (y + by) % 4)
                pairs.append(((x * 4 + y) * 2 + core, (to[0] * 4 + to[1]) * 2 + core))
    return pairs


def far_shift(by):
    return [(z, (z + 4 * by) % 16) for z in range(16)]


def column_shift(by):
    return [(z * 2 + c, (z + by[c]) % 16 * 2 + c) for z in range(16) for c in range(2)]


def second_axis_groups():
    place = [[[(x * 4 + y) * 2 + c for c in range(2)] for y in range(4)] for x in range(4)]
    along_y = [[place[j][i][0] for i in range(4)] for j in range(4)]
    along_x = [[place[i][j][1] for i in range(4)] for j in range(4)]
    return along_y + along_x


def first_axis_groups():
    place = [[[(x * 4 + y) * 2 + c for c in range(2)] for y in range(4)] for x in range(4)]
    along_x = [[place[i][j][0] for i in range(4)] for j in range(4)]
    along_y = [[place[j][i][1] for i in range(4)] for j in range(4)]
    return along_x + along_y


NEAR = ((1, 1), (2, -2), (-1, -1))


def per_device(inputs, weight, upstream, preactivation):
    core = lax.axis_index("core")
    info = jnp.stack([lax.axis_index(Z), core]).astype(jnp.int32)
    swap = [(0, 1), (1, 0)]

    slope = gelu_slope(preactivation.astype(jnp.float32))
    local = (upstream.astype(jnp.float32) * slope).astype(jnp.bfloat16)
    line = lax.all_gather(
        local, PLANE, axis=0, tiled=True, axis_index_groups=first_axis_groups()
    ).reshape(4, 32, 3072)
    inputs, line = lax.optimization_barrier((inputs, line))
    lines = lax.all_to_all(
        jnp.broadcast_to(line[None], (4, 4, 32, 3072)),
        PLANE,
        split_axis=0,
        concat_axis=0,
        tiled=True,
        axis_index_groups=second_axis_groups(),
    )
    near = [inputs] + [lax.ppermute(inputs, Z, far_shift(-d)) for d in (1, 2, 3)]
    lines, near = lax.optimization_barrier((lines, near))
    hg_own = lines.reshape(512, 3072)

    hg_sib = lax.ppermute(hg_own, "core", swap)
    sums = own_sums(hg_own, weight)
    own, *sends = sib_sums(info, sums, hg_sib, weight)
    own, near = lax.optimization_barrier((own, near))
    near = jnp.stack(near)
    nears = [near] + [lax.ppermute(near, Z + ("core",), column_shift(by)) for by in NEAR]
    received = [
        lax.ppermute(s, Z + ("core",), column_shift(by)) for s, by in zip(sends, NEAR)
    ]
    own, *sends = stage_sums(info, own, received)
    far = [lax.ppermute(s, Z, far_shift(d + 1)) for d, s in enumerate(sends)]
    weight_total = weight_sums(info, nears, hg_own, hg_sib)
    weight_total, *far = lax.optimization_barrier((weight_total, *far))
    return (final_sums(own, far), weight_total)


def solution(mesh):
    fine = Mesh(
        mesh.devices.reshape(4, 2, 4, 4, 2, 2), ("x", "yh", "zh", "zl", "yl", "core")
    )
    in_specs = (P(Z, PLANE), P(PLANE, Z), P(PLANE, Z), P(PLANE, Z))
    out_specs = (P(Z, PLANE), P(PLANE, Z))
    return jax.shard_map(
        per_device, mesh=fine, in_specs=in_specs, out_specs=out_specs, check_vma=False
    )
```

```python
import math

import jax
import jax.numpy as jnp
from jax import lax
from jax.experimental import pallas as pl
from jax.experimental.pallas import tpu as pltpu
from jax.sharding import Mesh
from jax.sharding import PartitionSpec as P

gelu_scale = math.sqrt(2.0 / math.pi)
cubic_term = 0.044715

MIB = 1024 * 1024
PLANE = ("x", "yh", "yl", "core")
Z = ("zh", "zl")
ROWS_BY_ROWS = (((1,), (1,)), ((), ()))


def gelu_slope(values):
    inner = gelu_scale * (values + cubic_term * values * values * values)
    tangent = jnp.tanh(inner)
    return 0.5 * (1.0 + tangent) + 0.5 * values * (1.0 - tangent * tangent) * gelu_scale * (
        1.0 + 3.0 * cubic_term * values * values
    )


def vmem():
    return pl.BlockSpec(memory_space=pltpu.VMEM)


def smem():
    return pl.BlockSpec(memory_space=pltpu.SMEM)


def block_rows(k):
    return pl.ds(pl.multiple_of(k * 32, 32), 32)


def place(core, x, y):
    return x * (1 + 3 * core) + y * (4 - 3 * core)


def own_kernel(lines_ref, w_ref, out_ref):
    out_ref[...] = lax.dot_general(
        lines_ref[...], w_ref[...], ROWS_BY_ROWS, preferred_element_type=jnp.float32
    )


def own_sums(lines, w):
    return pl.pallas_call(
        own_kernel,
        out_shape=jax.ShapeDtypeStruct((512, 384), jnp.float32),
        in_specs=[vmem()] * 2,
        out_specs=vmem(),
        compiler_params=pltpu.CompilerParams(vmem_limit_bytes=16 * MIB),
        cost_estimate=pl.CostEstimate(
            flops=2 * 512 * 3072 * 384, bytes_accessed=6 * MIB, transcendentals=0
        ),
        name="own_sums",
    )(lines, w)


def sib_kernel(info_ref, sums_ref, lines_ref, w_ref, own_ref, s1_ref, s2_ref, s3_ref, acc, chunks, sems):
    copies = [
        pltpu.make_async_copy(lines_ref.at[:, pl.ds(c * 768, 768)], chunks.at[c], sems.at[c])
        for c in range(4)
    ]
    for copy in copies:
        copy.start()
    for c, copy in enumerate(copies):
        copy.wait()
        part = lax.dot_general(
            chunks[c],
            w_ref[:, c * 768 : (c + 1) * 768],
            ROWS_BY_ROWS,
            preferred_element_type=jnp.float32,
        )
        acc[...] = part if c == 0 else acc[...] + part
    core = info_ref[1]
    for d, out in enumerate((own_ref, s1_ref, s2_ref, s3_ref)):
        residue = lax.rem(info_ref[0] + d, 4)
        for x in range(4):
            mine = sums_ref[block_rows(place(core, x, residue)), :]
            theirs = acc[block_rows(place(1 - core, x, residue)), :]
            out[x, block_rows(core), :] = mine.astype(out.dtype)
            out[x, block_rows(1 - core), :] = theirs.astype(out.dtype)


def sib_sums(info, sums, lines, w):
    shape = (4, 64, 384)
    return pl.pallas_call(
        sib_kernel,
        out_shape=[jax.ShapeDtypeStruct(shape, jnp.float32)]
        + [jax.ShapeDtypeStruct(shape, jnp.bfloat16)] * 3,
        in_specs=[smem(), vmem(), pl.BlockSpec(memory_space=pl.ANY), vmem()],
        out_specs=[vmem()] * 4,
        scratch_shapes=[
            pltpu.VMEM((512, 384), jnp.float32),
            pltpu.VMEM((4, 512, 768), jnp.bfloat16),
            pltpu.SemaphoreType.DMA((4,)),
        ],
        compiler_params=pltpu.CompilerParams(vmem_limit_bytes=16 * MIB),
        cost_estimate=pl.CostEstimate(
            flops=2 * 512 * 3072 * 384, bytes_accessed=8 * MIB, transcendentals=0
        ),
        name="sib_sums",
    )(info, sums, lines, w)


def stage_kernel(info_ref, own_ref, r1_ref, r2_ref, r3_ref, o_ref, s1_ref, s2_ref, s3_ref):
    zh = info_ref[0] // 4
    for d, out in enumerate((o_ref, s1_ref, s2_ref, s3_ref)):
        i = lax.rem(zh + d, 4)
        total = own_ref[i]
        for r in (r1_ref, r2_ref, r3_ref):
            total = total + r[i].astype(jnp.float32)
        out[...] = total.astype(out.dtype)


def stage_sums(info, own, received):
    shape = (64, 384)
    return pl.pallas_call(
        stage_kernel,
        out_shape=[jax.ShapeDtypeStruct(shape, jnp.float32)]
        + [jax.ShapeDtypeStruct(shape, jnp.bfloat16)] * 3,
        in_specs=[smem()] + [vmem()] * 4,
        out_specs=[vmem()] * 4,
        compiler_params=pltpu.CompilerParams(vmem_limit_bytes=16 * MIB),
        cost_estimate=pl.CostEstimate(flops=400000, bytes_accessed=2 * MIB, transcendentals=0),
        name="stage_sums",
    )(info, own, *received)


def final_kernel(own_ref, r1_ref, r2_ref, r3_ref, out_ref):
    total = own_ref[...]
    for r in (r1_ref, r2_ref, r3_ref):
        total = total + r[...].astype(jnp.float32)
    out_ref[...] = total.astype(jnp.bfloat16)


def final_sums(own, received):
    return pl.pallas_call(
        final_kernel,
        out_shape=jax.ShapeDtypeStruct((64, 384), jnp.bfloat16),
        in_specs=[vmem()] * 4,
        out_specs=vmem(),
        compiler_params=pltpu.CompilerParams(vmem_limit_bytes=4 * MIB),
        cost_estimate=pl.CostEstimate(flops=100000, bytes_accessed=MIB // 4, transcendentals=0),
        name="final_sums",
    )(own, *received)


def weight_kernel(info_ref, n0_ref, n1_ref, n2_ref, n3_ref, own_ref, sib_ref, out_ref, tokens, left):

    @pl.when(pl.program_id(0) == 0)
    def _():
        z, core = info_ref[0], info_ref[1]
        for ref, far in ((n0_ref, 0), (n1_ref, -1), (n2_ref, 4 * core - 2), (n3_ref, 1)):
            for e in range(4):
                k = lax.rem(z + far + 4 * e + 16, 16)
                for which in range(2):
                    half = core if which == 0 else 1 - core
                    at = place(half, k // 4, lax.rem(k, 4))
                    rows = pl.ds(pl.multiple_of(which * 512 + at * 32, 32), 32)
                    tokens[rows, :] = ref[e, pl.ds(pl.multiple_of(half * 32, 32), 32), :]
        left[...] = tokens[...].T

    total = jnp.dot(left[:, :512], own_ref[...], preferred_element_type=jnp.float32)
    total += jnp.dot(left[:, 512:], sib_ref[...], preferred_element_type=jnp.float32)
    out_ref[...] = total.astype(jnp.bfloat16)


def weight_sums(info, near, hg_own, hg_sib):
    tile = 512
    return pl.pallas_call(
        weight_kernel,
        out_shape=jax.ShapeDtypeStruct((384, 3072), jnp.bfloat16),
        grid_spec=pltpu.PrefetchScalarGridSpec(
            num_scalar_prefetch=1,
            grid=(3072 // tile,),
            in_specs=[pl.BlockSpec((4, 64, 384), lambda j, info: (0, 0, 0))] * 4
            + [pl.BlockSpec((512, tile), lambda j, info: (0, j))] * 2,
            out_specs=pl.BlockSpec((384, tile), lambda j, info: (0, j)),
            scratch_shapes=[
                pltpu.VMEM((1024, 384), jnp.bfloat16),
                pltpu.VMEM((384, 1024), jnp.bfloat16),
            ],
        ),
        compiler_params=pltpu.CompilerParams(vmem_limit_bytes=24 * MIB),
        cost_estimate=pl.CostEstimate(
            flops=2 * 1024 * 3072 * 384, bytes_accessed=10 * MIB, transcendentals=0
        ),
        name="weight_sums",
    )(info, *near, hg_own, hg_sib)


def plane_shift(first, by):
    pairs = []
    for x in range(4):
        for y in range(4):
            for core in range(2):
                along_x = (core == 0) == first
                to = ((x + by) % 4, y) if along_x else (x, (y + by) % 4)
                pairs.append(((x * 4 + y) * 2 + core, (to[0] * 4 + to[1]) * 2 + core))
    return pairs


def far_shift(by):
    return [(z, (z + 4 * by) % 16) for z in range(16)]


def column_shift(by):
    return [(z * 2 + c, (z + by[c]) % 16 * 2 + c) for z in range(16) for c in range(2)]


def second_axis_groups():
    place = [[[(x * 4 + y) * 2 + c for c in range(2)] for y in range(4)] for x in range(4)]
    along_y = [[place[j][i][0] for i in range(4)] for j in range(4)]
    along_x = [[place[i][j][1] for i in range(4)] for j in range(4)]
    return along_y + along_x


def first_axis_groups():
    place = [[[(x * 4 + y) * 2 + c for c in range(2)] for y in range(4)] for x in range(4)]
    along_x = [[place[i][j][0] for i in range(4)] for j in range(4)]
    along_y = [[place[j][i][1] for i in range(4)] for j in range(4)]
    return along_x + along_y


NEAR = ((1, 1), (2, -2), (-1, -1))


def per_device(inputs, weight, upstream, preactivation):
    core = lax.axis_index("core")
    info = jnp.stack([lax.axis_index(Z), core]).astype(jnp.int32)
    swap = [(0, 1), (1, 0)]

    slope = gelu_slope(preactivation.astype(jnp.float32))
    local = (upstream.astype(jnp.float32) * slope).astype(jnp.bfloat16)
    line = lax.all_gather(
        local, PLANE, axis=0, tiled=True, axis_index_groups=first_axis_groups()
    ).reshape(4, 32, 3072)
    inputs, line = lax.optimization_barrier((inputs, line))
    lines = lax.all_to_all(
        jnp.broadcast_to(line[None], (4, 4, 32, 3072)),
        PLANE,
        split_axis=0,
        concat_axis=0,
        tiled=True,
        axis_index_groups=second_axis_groups(),
    )
    near = [inputs] + [lax.ppermute(inputs, Z, far_shift(-d)) for d in (1, 2, 3)]
    lines, near = lax.optimization_barrier((lines, near))
    hg_own = lines.reshape(512, 3072)

    hg_sib = lax.ppermute(hg_own, "core", swap)
    near = jnp.stack(near)
    first = lax.ppermute(near, Z + ("core",), column_shift(NEAR[0]))
    sums = own_sums(hg_own, weight)
    sums, first = lax.optimization_barrier((sums, first))
    own, *sends = sib_sums(info, sums, hg_sib, weight)
    own, near = lax.optimization_barrier((own, near))
    nears = [near, first]
    nears += [lax.ppermute(near, Z + ("core",), column_shift(by)) for by in NEAR[1:]]
    received = [
        lax.ppermute(s, Z + ("core",), column_shift(by)) for s, by in zip(sends, NEAR)
    ]
    own, *sends = stage_sums(info, own, received)
    far = [lax.ppermute(s, Z, far_shift(d + 1)) for d, s in enumerate(sends)]
    weight_total = weight_sums(info, nears, hg_own, hg_sib)
    weight_total, *far = lax.optimization_barrier((weight_total, *far))
    return (final_sums(own, far), weight_total)


def solution(mesh):
    fine = Mesh(
        mesh.devices.reshape(4, 2, 4, 4, 2, 2), ("x", "yh", "zh", "zl", "yl", "core")
    )
    in_specs = (P(Z, PLANE), P(PLANE, Z), P(PLANE, Z), P(PLANE, Z))
    out_specs = (P(Z, PLANE), P(PLANE, Z))
    return jax.shard_map(
        per_device, mesh=fine, in_specs=in_specs, out_specs=out_specs, check_vma=False
    )
```

```python
import math

import jax
import jax.numpy as jnp
from jax import lax
from jax.experimental import pallas as pl
from jax.experimental.pallas import tpu as pltpu
from jax.sharding import Mesh
from jax.sharding import PartitionSpec as P

gelu_scale = math.sqrt(2.0 / math.pi)
cubic_term = 0.044715

MIB = 1024 * 1024
PLANE = ("x", "yh", "yl", "core")
Z = ("zh", "zl")
ROWS_BY_ROWS = (((1,), (1,)), ((), ()))


def gelu_slope(values):
    inner = gelu_scale * (values + cubic_term * values * values * values)
    tangent = jnp.tanh(inner)
    return 0.5 * (1.0 + tangent) + 0.5 * values * (1.0 - tangent * tangent) * gelu_scale * (
        1.0 + 3.0 * cubic_term * values * values
    )


def vmem():
    return pl.BlockSpec(memory_space=pltpu.VMEM)


def smem():
    return pl.BlockSpec(memory_space=pltpu.SMEM)


def block_rows(k):
    return pl.ds(pl.multiple_of(k * 32, 32), 32)


def place(core, x, y):
    return x * (1 + 3 * core) + y * (4 - 3 * core)


def own_kernel(lines_ref, w_ref, out_ref):
    out_ref[...] = lax.dot_general(
        lines_ref[...], w_ref[...], ROWS_BY_ROWS, preferred_element_type=jnp.float32
    )


def own_sums(lines, w):
    return pl.pallas_call(
        own_kernel,
        out_shape=jax.ShapeDtypeStruct((512, 384), jnp.float32),
        in_specs=[vmem()] * 2,
        out_specs=vmem(),
        compiler_params=pltpu.CompilerParams(vmem_limit_bytes=16 * MIB),
        cost_estimate=pl.CostEstimate(
            flops=2 * 512 * 3072 * 384, bytes_accessed=6 * MIB, transcendentals=0
        ),
        name="own_sums",
    )(lines, w)


def sib_kernel(info_ref, sums_ref, lines_ref, w_ref, own_ref, s1_ref, s2_ref, s3_ref, acc):
    acc[...] = lax.dot_general(
        lines_ref[...], w_ref[...], ROWS_BY_ROWS, preferred_element_type=jnp.float32
    )
    core = info_ref[1]
    for d, out in enumerate((own_ref, s1_ref, s2_ref, s3_ref)):
        residue = lax.rem(info_ref[0] + d, 4)
        for x in range(4):
            mine = sums_ref[block_rows(place(core, x, residue)), :]
            theirs = acc[block_rows(place(1 - core, x, residue)), :]
            out[x, block_rows(core), :] = mine.astype(out.dtype)
            out[x, block_rows(1 - core), :] = theirs.astype(out.dtype)


def sib_sums(info, sums, lines, w):
    shape = (4, 64, 384)
    return pl.pallas_call(
        sib_kernel,
        out_shape=[jax.ShapeDtypeStruct(shape, jnp.float32)]
        + [jax.ShapeDtypeStruct(shape, jnp.bfloat16)] * 3,
        in_specs=[smem()] + [vmem()] * 3,
        out_specs=[vmem()] * 4,
        scratch_shapes=[pltpu.VMEM((512, 384), jnp.float32)],
        compiler_params=pltpu.CompilerParams(vmem_limit_bytes=16 * MIB),
        cost_estimate=pl.CostEstimate(
            flops=2 * 512 * 3072 * 384, bytes_accessed=8 * MIB, transcendentals=0
        ),
        name="sib_sums",
    )(info, sums, lines, w)


def stage_kernel(info_ref, own_ref, r1_ref, r2_ref, r3_ref, o_ref, s1_ref, s2_ref, s3_ref):
    zh = info_ref[0] // 4
    for d, out in enumerate((o_ref, s1_ref, s2_ref, s3_ref)):
        i = lax.rem(zh + d, 4)
        total = own_ref[i]
        for r in (r1_ref, r2_ref, r3_ref):
            total = total + r[i].astype(jnp.float32)
        out[...] = total.astype(out.dtype)


def stage_sums(info, own, received):
    shape = (64, 384)
    return pl.pallas_call(
        stage_kernel,
        out_shape=[jax.ShapeDtypeStruct(shape, jnp.float32)]
        + [jax.ShapeDtypeStruct(shape, jnp.bfloat16)] * 3,
        in_specs=[smem()] + [vmem()] * 4,
        out_specs=[vmem()] * 4,
        compiler_params=pltpu.CompilerParams(vmem_limit_bytes=16 * MIB),
        cost_estimate=pl.CostEstimate(flops=400000, bytes_accessed=2 * MIB, transcendentals=0),
        name="stage_sums",
    )(info, own, *received)


def final_kernel(own_ref, r1_ref, r2_ref, r3_ref, out_ref):
    total = own_ref[...]
    for r in (r1_ref, r2_ref, r3_ref):
        total = total + r[...].astype(jnp.float32)
    out_ref[...] = total.astype(jnp.bfloat16)


def final_sums(own, received):
    return pl.pallas_call(
        final_kernel,
        out_shape=jax.ShapeDtypeStruct((64, 384), jnp.bfloat16),
        in_specs=[vmem()] * 4,
        out_specs=vmem(),
        compiler_params=pltpu.CompilerParams(vmem_limit_bytes=4 * MIB),
        cost_estimate=pl.CostEstimate(flops=100000, bytes_accessed=MIB // 4, transcendentals=0),
        name="final_sums",
    )(own, *received)


def weight_kernel(info_ref, n0_ref, n1_ref, n2_ref, n3_ref, own_ref, sib_ref, out_ref, tokens, left):

    @pl.when(pl.program_id(0) == 0)
    def _():
        z, core = info_ref[0], info_ref[1]
        for ref, far in ((n0_ref, 0), (n1_ref, -1), (n2_ref, 4 * core - 2), (n3_ref, 1)):
            for e in range(4):
                k = lax.rem(z + far + 4 * e + 16, 16)
                for which in range(2):
                    half = core if which == 0 else 1 - core
                    at = place(half, k // 4, lax.rem(k, 4))
                    rows = pl.ds(pl.multiple_of(which * 512 + at * 32, 32), 32)
                    tokens[rows, :] = ref[e, pl.ds(pl.multiple_of(half * 32, 32), 32), :]
        left[...] = tokens[...].T

    total = jnp.dot(left[:, :512], own_ref[...], preferred_element_type=jnp.float32)
    total += jnp.dot(left[:, 512:], sib_ref[...], preferred_element_type=jnp.float32)
    out_ref[...] = total.astype(jnp.bfloat16)


def weight_sums(info, near, hg_own, hg_sib):
    tile = 512
    return pl.pallas_call(
        weight_kernel,
        out_shape=jax.ShapeDtypeStruct((384, 3072), jnp.bfloat16),
        grid_spec=pltpu.PrefetchScalarGridSpec(
            num_scalar_prefetch=1,
            grid=(3072 // tile,),
            in_specs=[pl.BlockSpec((4, 64, 384), lambda j, info: (0, 0, 0))] * 4
            + [pl.BlockSpec((512, tile), lambda j, info: (0, j))] * 2,
            out_specs=pl.BlockSpec((384, tile), lambda j, info: (0, j)),
            scratch_shapes=[
                pltpu.VMEM((1024, 384), jnp.bfloat16),
                pltpu.VMEM((384, 1024), jnp.bfloat16),
            ],
        ),
        compiler_params=pltpu.CompilerParams(vmem_limit_bytes=24 * MIB),
        cost_estimate=pl.CostEstimate(
            flops=2 * 1024 * 3072 * 384, bytes_accessed=10 * MIB, transcendentals=0
        ),
        name="weight_sums",
    )(info, *near, hg_own, hg_sib)


def plane_shift(first, by):
    pairs = []
    for x in range(4):
        for y in range(4):
            for core in range(2):
                along_x = (core == 0) == first
                to = ((x + by) % 4, y) if along_x else (x, (y + by) % 4)
                pairs.append(((x * 4 + y) * 2 + core, (to[0] * 4 + to[1]) * 2 + core))
    return pairs


def far_shift(by):
    return [(z, (z + 4 * by) % 16) for z in range(16)]


def column_shift(by):
    return [(z * 2 + c, (z + by[c]) % 16 * 2 + c) for z in range(16) for c in range(2)]


def second_axis_groups():
    place = [[[(x * 4 + y) * 2 + c for c in range(2)] for y in range(4)] for x in range(4)]
    along_y = [[place[j][i][0] for i in range(4)] for j in range(4)]
    along_x = [[place[i][j][1] for i in range(4)] for j in range(4)]
    return along_y + along_x


def first_axis_groups():
    place = [[[(x * 4 + y) * 2 + c for c in range(2)] for y in range(4)] for x in range(4)]
    along_x = [[place[i][j][0] for i in range(4)] for j in range(4)]
    along_y = [[place[j][i][1] for i in range(4)] for j in range(4)]
    return along_x + along_y


NEAR = ((1, 1), (2, -2), (-1, -1))


def per_device(inputs, weight, upstream, preactivation):
    core = lax.axis_index("core")
    info = jnp.stack([lax.axis_index(Z), core]).astype(jnp.int32)
    swap = [(0, 1), (1, 0)]

    slope = gelu_slope(preactivation.astype(jnp.float32))
    local = (upstream.astype(jnp.float32) * slope).astype(jnp.bfloat16)
    line = lax.all_to_all(
        jnp.broadcast_to(local[None], (4, 32, 3072)),
        PLANE,
        split_axis=0,
        concat_axis=0,
        tiled=True,
        axis_index_groups=first_axis_groups(),
    )
    inputs, line = lax.optimization_barrier((inputs, line))
    lines = lax.all_to_all(
        jnp.broadcast_to(line[None], (4, 4, 32, 3072)),
        PLANE,
        split_axis=0,
        concat_axis=0,
        tiled=True,
        axis_index_groups=second_axis_groups(),
    )
    near = [inputs] + [lax.ppermute(inputs, Z, far_shift(-d)) for d in (1, 2, 3)]
    lines, near = lax.optimization_barrier((lines, near))
    hg_own = lines.reshape(512, 3072)

    hg_sib = lax.ppermute(hg_own, "core", swap)
    sums = own_sums(hg_own, weight)
    own, *sends = sib_sums(info, sums, hg_sib, weight)
    own, near = lax.optimization_barrier((own, near))
    near = jnp.stack(near)
    nears = [near] + [lax.ppermute(near, Z + ("core",), column_shift(by)) for by in NEAR]
    received = [
        lax.ppermute(s, Z + ("core",), column_shift(by)) for s, by in zip(sends, NEAR)
    ]
    own, *sends = stage_sums(info, own, received)
    far = [lax.ppermute(s, Z, far_shift(d + 1)) for d, s in enumerate(sends)]
    weight_total = weight_sums(info, nears, hg_own, hg_sib)
    weight_total, *far = lax.optimization_barrier((weight_total, *far))
    return (final_sums(own, far), weight_total)


def solution(mesh):
    fine = Mesh(
        mesh.devices.reshape(4, 2, 4, 4, 2, 2), ("x", "yh", "zh", "zl", "yl", "core")
    )
    in_specs = (P(Z, PLANE), P(PLANE, Z), P(PLANE, Z), P(PLANE, Z))
    out_specs = (P(Z, PLANE), P(PLANE, Z))
    return jax.shard_map(
        per_device, mesh=fine, in_specs=in_specs, out_specs=out_specs, check_vma=False
    )
```

```python
import math

import jax
import jax.numpy as jnp
from jax import lax
from jax.experimental import pallas as pl
from jax.experimental.pallas import tpu as pltpu
from jax.sharding import Mesh
from jax.sharding import PartitionSpec as P

gelu_scale = math.sqrt(2.0 / math.pi)
cubic_term = 0.044715

MIB = 1024 * 1024
PLANE = ("x", "yh", "yl", "core")
Z = ("zh", "zl")
ROWS_BY_ROWS = (((1,), (1,)), ((), ()))


def gelu_slope(values):
    inner = gelu_scale * (values + cubic_term * values * values * values)
    tangent = jnp.tanh(inner)
    return 0.5 * (1.0 + tangent) + 0.5 * values * (1.0 - tangent * tangent) * gelu_scale * (
        1.0 + 3.0 * cubic_term * values * values
    )


def vmem():
    return pl.BlockSpec(memory_space=pltpu.VMEM)


def smem():
    return pl.BlockSpec(memory_space=pltpu.SMEM)


def block_rows(k):
    return pl.ds(pl.multiple_of(k * 32, 32), 32)


def place(core, x, y):
    return x * (1 + 3 * core) + y * (4 - 3 * core)


def own_kernel(lines_ref, w_ref, out_ref):
    out_ref[...] = lax.dot_general(
        lines_ref[...], w_ref[...], ROWS_BY_ROWS, preferred_element_type=jnp.float32
    )


def own_sums(lines, w):
    return pl.pallas_call(
        own_kernel,
        out_shape=jax.ShapeDtypeStruct((512, 384), jnp.float32),
        in_specs=[vmem()] * 2,
        out_specs=vmem(),
        compiler_params=pltpu.CompilerParams(vmem_limit_bytes=16 * MIB),
        cost_estimate=pl.CostEstimate(
            flops=2 * 512 * 3072 * 384, bytes_accessed=6 * MIB, transcendentals=0
        ),
        name="own_sums",
    )(lines, w)


def sib_kernel(info_ref, sums_ref, lines_ref, w_ref, own_ref, s1_ref, s2_ref, s3_ref, acc):
    acc[...] = lax.dot_general(
        lines_ref[...], w_ref[...], ROWS_BY_ROWS, preferred_element_type=jnp.float32
    )
    core = info_ref[1]
    for d, out in enumerate((own_ref, s1_ref, s2_ref, s3_ref)):
        residue = lax.rem(info_ref[0] + d, 4)
        for x in range(4):
            mine = sums_ref[block_rows(place(core, x, residue)), :]
            theirs = acc[block_rows(place(1 - core, x, residue)), :]
            out[x, block_rows(core), :] = mine.astype(out.dtype)
            out[x, block_rows(1 - core), :] = theirs.astype(out.dtype)


def sib_sums(info, sums, lines, w):
    shape = (4, 64, 384)
    return pl.pallas_call(
        sib_kernel,
        out_shape=[jax.ShapeDtypeStruct(shape, jnp.float32)]
        + [jax.ShapeDtypeStruct(shape, jnp.bfloat16)] * 3,
        in_specs=[smem()] + [vmem()] * 3,
        out_specs=[vmem()] * 4,
        scratch_shapes=[pltpu.VMEM((512, 384), jnp.float32)],
        compiler_params=pltpu.CompilerParams(vmem_limit_bytes=16 * MIB),
        cost_estimate=pl.CostEstimate(
            flops=2 * 512 * 3072 * 384, bytes_accessed=8 * MIB, transcendentals=0
        ),
        name="sib_sums",
    )(info, sums, lines, w)


def stage_kernel(info_ref, own_ref, r1_ref, r2_ref, r3_ref, o_ref, s1_ref, s2_ref, s3_ref):
    zh = info_ref[0] // 4
    for d, out in enumerate((o_ref, s1_ref, s2_ref, s3_ref)):
        i = lax.rem(zh + d, 4)
        total = own_ref[i]
        for r in (r1_ref, r2_ref, r3_ref):
            total = total + r[i].astype(jnp.float32)
        out[...] = total.astype(out.dtype)


def stage_sums(info, own, received):
    shape = (64, 384)
    return pl.pallas_call(
        stage_kernel,
        out_shape=[jax.ShapeDtypeStruct(shape, jnp.float32)]
        + [jax.ShapeDtypeStruct(shape, jnp.bfloat16)] * 3,
        in_specs=[smem()] + [vmem()] * 4,
        out_specs=[vmem()] * 4,
        compiler_params=pltpu.CompilerParams(vmem_limit_bytes=16 * MIB),
        cost_estimate=pl.CostEstimate(flops=400000, bytes_accessed=2 * MIB, transcendentals=0),
        name="stage_sums",
    )(info, own, *received)


def final_kernel(own_ref, r1_ref, r2_ref, r3_ref, out_ref):
    total = own_ref[...]
    for r in (r1_ref, r2_ref, r3_ref):
        total = total + r[...].astype(jnp.float32)
    out_ref[...] = total.astype(jnp.bfloat16)


def final_sums(own, received):
    return pl.pallas_call(
        final_kernel,
        out_shape=jax.ShapeDtypeStruct((64, 384), jnp.bfloat16),
        in_specs=[vmem()] * 4,
        out_specs=vmem(),
        compiler_params=pltpu.CompilerParams(vmem_limit_bytes=4 * MIB),
        cost_estimate=pl.CostEstimate(flops=100000, bytes_accessed=MIB // 4, transcendentals=0),
        name="final_sums",
    )(own, *received)


def weight_kernel(info_ref, n0_ref, n1_ref, n2_ref, n3_ref, own_ref, sib_ref, out_ref, tokens, left):

    @pl.when(pl.program_id(0) == 0)
    def _():
        z, core = info_ref[0], info_ref[1]
        for ref, far in ((n0_ref, 0), (n1_ref, -1), (n2_ref, 4 * core - 2), (n3_ref, 1)):
            for e in range(4):
                k = lax.rem(z + far + 4 * e + 16, 16)
                for which in range(2):
                    half = core if which == 0 else 1 - core
                    at = place(half, k // 4, lax.rem(k, 4))
                    rows = pl.ds(pl.multiple_of(which * 512 + at * 32, 32), 32)
                    tokens[rows, :] = ref[e, pl.ds(pl.multiple_of(half * 32, 32), 32), :]
        left[...] = tokens[...].T

    total = jnp.dot(left[:, :512], own_ref[...], preferred_element_type=jnp.float32)
    total += jnp.dot(left[:, 512:], sib_ref[...], preferred_element_type=jnp.float32)
    out_ref[...] = total.astype(jnp.bfloat16)


def weight_sums(info, near, hg_own, hg_sib):
    tile = 1024
    return pl.pallas_call(
        weight_kernel,
        out_shape=jax.ShapeDtypeStruct((384, 3072), jnp.bfloat16),
        grid_spec=pltpu.PrefetchScalarGridSpec(
            num_scalar_prefetch=1,
            grid=(3072 // tile,),
            in_specs=[pl.BlockSpec((4, 64, 384), lambda j, info: (0, 0, 0))] * 4
            + [pl.BlockSpec((512, tile), lambda j, info: (0, j))] * 2,
            out_specs=pl.BlockSpec((384, tile), lambda j, info: (0, j)),
            scratch_shapes=[
                pltpu.VMEM((1024, 384), jnp.bfloat16),
                pltpu.VMEM((384, 1024), jnp.bfloat16),
            ],
        ),
        compiler_params=pltpu.CompilerParams(vmem_limit_bytes=24 * MIB),
        cost_estimate=pl.CostEstimate(
            flops=2 * 1024 * 3072 * 384, bytes_accessed=10 * MIB, transcendentals=0
        ),
        name="weight_sums",
    )(info, *near, hg_own, hg_sib)


def plane_shift(first, by):
    pairs = []
    for x in range(4):
        for y in range(4):
            for core in range(2):
                along_x = (core == 0) == first
                to = ((x + by) % 4, y) if along_x else (x, (y + by) % 4)
                pairs.append(((x * 4 + y) * 2 + core, (to[0] * 4 + to[1]) * 2 + core))
    return pairs


def far_shift(by):
    return [(z, (z + 4 * by) % 16) for z in range(16)]


def column_shift(by):
    return [(z * 2 + c, (z + by[c]) % 16 * 2 + c) for z in range(16) for c in range(2)]


def second_axis_groups():
    place = [[[(x * 4 + y) * 2 + c for c in range(2)] for y in range(4)] for x in range(4)]
    along_y = [[place[j][i][0] for i in range(4)] for j in range(4)]
    along_x = [[place[i][j][1] for i in range(4)] for j in range(4)]
    return along_y + along_x


def first_axis_groups():
    place = [[[(x * 4 + y) * 2 + c for c in range(2)] for y in range(4)] for x in range(4)]
    along_x = [[place[i][j][0] for i in range(4)] for j in range(4)]
    along_y = [[place[j][i][1] for i in range(4)] for j in range(4)]
    return along_x + along_y


NEAR = ((1, 1), (2, -2), (-1, -1))


def per_device(inputs, weight, upstream, preactivation):
    core = lax.axis_index("core")
    info = jnp.stack([lax.axis_index(Z), core]).astype(jnp.int32)
    swap = [(0, 1), (1, 0)]

    slope = gelu_slope(preactivation.astype(jnp.float32))
    local = (upstream.astype(jnp.float32) * slope).astype(jnp.bfloat16)
    line = lax.all_gather(
        local, PLANE, axis=0, tiled=True, axis_index_groups=first_axis_groups()
    ).reshape(4, 32, 3072)
    inputs, line = lax.optimization_barrier((inputs, line))
    lines = lax.all_to_all(
        jnp.broadcast_to(line[None], (4, 4, 32, 3072)),
        PLANE,
        split_axis=0,
        concat_axis=0,
        tiled=True,
        axis_index_groups=second_axis_groups(),
    )
    near = [inputs] + [lax.ppermute(inputs, Z, far_shift(-d)) for d in (1, 2, 3)]
    lines, near = lax.optimization_barrier((lines, near))
    hg_own = lines.reshape(512, 3072)

    hg_sib = lax.ppermute(hg_own, "core", swap)
    sums = own_sums(hg_own, weight)
    own, *sends = sib_sums(info, sums, hg_sib, weight)
    own, near = lax.optimization_barrier((own, near))
    near = jnp.stack(near)
    nears = [near] + [lax.ppermute(near, Z + ("core",), column_shift(by)) for by in NEAR]
    received = [
        lax.ppermute(s, Z + ("core",), column_shift(by)) for s, by in zip(sends, NEAR)
    ]
    own, *sends = stage_sums(info, own, received)
    far = [lax.ppermute(s, Z, far_shift(d + 1)) for d, s in enumerate(sends)]
    weight_total = weight_sums(info, nears, hg_own, hg_sib)
    weight_total, *far = lax.optimization_barrier((weight_total, *far))
    return (final_sums(own, far), weight_total)


def solution(mesh):
    fine = Mesh(
        mesh.devices.reshape(4, 2, 4, 4, 2, 2), ("x", "yh", "zh", "zl", "yl", "core")
    )
    in_specs = (P(Z, PLANE), P(PLANE, Z), P(PLANE, Z), P(PLANE, Z))
    out_specs = (P(Z, PLANE), P(PLANE, Z))
    return jax.shard_map(
        per_device, mesh=fine, in_specs=in_specs, out_specs=out_specs, check_vma=False
    )
```

```python
import math

import jax
import jax.numpy as jnp
from jax import lax
from jax.experimental import pallas as pl
from jax.experimental.pallas import tpu as pltpu
from jax.sharding import Mesh
from jax.sharding import PartitionSpec as P

gelu_scale = math.sqrt(2.0 / math.pi)
cubic_term = 0.044715

MIB = 1024 * 1024
PLANE = ("x", "yh", "yl", "core")
Z = ("zh", "zl")
ROWS_BY_ROWS = (((1,), (1,)), ((), ()))


def gelu_slope(values):
    inner = gelu_scale * (values + cubic_term * values * values * values)
    tangent = jnp.tanh(inner)
    return 0.5 * (1.0 + tangent) + 0.5 * values * (1.0 - tangent * tangent) * gelu_scale * (
        1.0 + 3.0 * cubic_term * values * values
    )


def vmem():
    return pl.BlockSpec(memory_space=pltpu.VMEM)


def smem():
    return pl.BlockSpec(memory_space=pltpu.SMEM)


def block_rows(k):
    return pl.ds(pl.multiple_of(k * 32, 32), 32)


def place(core, x, y):
    return x * (1 + 3 * core) + y * (4 - 3 * core)


def own_kernel(lines_ref, w_ref, out_ref):
    out_ref[...] = lax.dot_general(
        lines_ref[...], w_ref[...], ROWS_BY_ROWS, preferred_element_type=jnp.float32
    )


def own_sums(lines, w):
    return pl.pallas_call(
        own_kernel,
        out_shape=jax.ShapeDtypeStruct((512, 384), jnp.float32),
        in_specs=[vmem()] * 2,
        out_specs=vmem(),
        compiler_params=pltpu.CompilerParams(vmem_limit_bytes=16 * MIB),
        cost_estimate=pl.CostEstimate(
            flops=2 * 512 * 3072 * 384, bytes_accessed=6 * MIB, transcendentals=0
        ),
        name="own_sums",
    )(lines, w)


def sib_kernel(info_ref, sums_ref, lines_ref, w_ref, own_ref, s1_ref, s2_ref, s3_ref, acc):
    acc[...] = lax.dot_general(
        lines_ref[...], w_ref[...], ROWS_BY_ROWS, preferred_element_type=jnp.float32
    )
    core = info_ref[1]
    for d, out in enumerate((own_ref, s1_ref, s2_ref, s3_ref)):
        residue = lax.rem(info_ref[0] + d, 4)
        for x in range(4):
            mine = sums_ref[block_rows(place(core, x, residue)), :]
            theirs = acc[block_rows(place(1 - core, x, residue)), :]
            out[x, block_rows(core), :] = mine.astype(out.dtype)
            out[x, block_rows(1 - core), :] = theirs.astype(out.dtype)


def sib_sums(info, sums, lines, w):
    shape = (4, 64, 384)
    return pl.pallas_call(
        sib_kernel,
        out_shape=[jax.ShapeDtypeStruct(shape, jnp.float32)]
        + [jax.ShapeDtypeStruct(shape, jnp.bfloat16)] * 3,
        in_specs=[smem()] + [vmem()] * 3,
        out_specs=[vmem()] * 4,
        scratch_shapes=[pltpu.VMEM((512, 384), jnp.float32)],
        compiler_params=pltpu.CompilerParams(vmem_limit_bytes=16 * MIB),
        cost_estimate=pl.CostEstimate(
            flops=2 * 512 * 3072 * 384, bytes_accessed=8 * MIB, transcendentals=0
        ),
        name="sib_sums",
    )(info, sums, lines, w)


def stage_kernel(info_ref, own_ref, r1_ref, r2_ref, r3_ref, o_ref, s1_ref, s2_ref, s3_ref):
    zh = info_ref[0] // 4
    for d, out in enumerate((o_ref, s1_ref, s2_ref, s3_ref)):
        i = lax.rem(zh + d, 4)
        total = own_ref[i]
        for r in (r1_ref, r2_ref, r3_ref):
            total = total + r[i].astype(jnp.float32)
        out[...] = total.astype(out.dtype)


def stage_sums(info, own, received):
    shape = (64, 384)
    return pl.pallas_call(
        stage_kernel,
        out_shape=[jax.ShapeDtypeStruct(shape, jnp.float32)]
        + [jax.ShapeDtypeStruct(shape, jnp.bfloat16)] * 3,
        in_specs=[smem()] + [vmem()] * 4,
        out_specs=[vmem()] * 4,
        compiler_params=pltpu.CompilerParams(vmem_limit_bytes=16 * MIB),
        cost_estimate=pl.CostEstimate(flops=400000, bytes_accessed=2 * MIB, transcendentals=0),
        name="stage_sums",
    )(info, own, *received)


def final_kernel(own_ref, r1_ref, r2_ref, r3_ref, out_ref):
    total = own_ref[...]
    for r in (r1_ref, r2_ref, r3_ref):
        total = total + r[...].astype(jnp.float32)
    out_ref[...] = total.astype(jnp.bfloat16)


def final_sums(own, received):
    return pl.pallas_call(
        final_kernel,
        out_shape=jax.ShapeDtypeStruct((64, 384), jnp.bfloat16),
        in_specs=[vmem()] * 4,
        out_specs=vmem(),
        compiler_params=pltpu.CompilerParams(vmem_limit_bytes=4 * MIB),
        cost_estimate=pl.CostEstimate(flops=100000, bytes_accessed=MIB // 4, transcendentals=0),
        name="final_sums",
    )(own, *received)


def weight_kernel(info_ref, n0_ref, n1_ref, n2_ref, n3_ref, own_ref, sib_ref, out_ref, tokens, left):

    @pl.when(pl.program_id(0) == 0)
    def _():
        z, core = info_ref[0], info_ref[1]
        for ref, far in ((n0_ref, 0), (n1_ref, -1), (n2_ref, 4 * core - 2), (n3_ref, 1)):
            for e in range(4):
                k = lax.rem(z + far + 4 * e + 16, 16)
                for which in range(2):
                    half = core if which == 0 else 1 - core
                    at = place(half, k // 4, lax.rem(k, 4))
                    rows = pl.ds(pl.multiple_of(which * 512 + at * 32, 32), 32)
                    tokens[rows, :] = ref[e, pl.ds(pl.multiple_of(half * 32, 32), 32), :]
        left[...] = tokens[...].T

    total = jnp.dot(left[:, :512], own_ref[...], preferred_element_type=jnp.float32)
    total += jnp.dot(left[:, 512:], sib_ref[...], preferred_element_type=jnp.float32)
    out_ref[...] = total.astype(jnp.bfloat16)


def weight_sums(info, near, hg_own, hg_sib):
    tile = 1536
    return pl.pallas_call(
        weight_kernel,
        out_shape=jax.ShapeDtypeStruct((384, 3072), jnp.bfloat16),
        grid_spec=pltpu.PrefetchScalarGridSpec(
            num_scalar_prefetch=1,
            grid=(3072 // tile,),
            in_specs=[pl.BlockSpec((4, 64, 384), lambda j, info: (0, 0, 0))] * 4
            + [pl.BlockSpec((512, tile), lambda j, info: (0, j))] * 2,
            out_specs=pl.BlockSpec((384, tile), lambda j, info: (0, j)),
            scratch_shapes=[
                pltpu.VMEM((1024, 384), jnp.bfloat16),
                pltpu.VMEM((384, 1024), jnp.bfloat16),
            ],
        ),
        compiler_params=pltpu.CompilerParams(vmem_limit_bytes=24 * MIB),
        cost_estimate=pl.CostEstimate(
            flops=2 * 1024 * 3072 * 384, bytes_accessed=10 * MIB, transcendentals=0
        ),
        name="weight_sums",
    )(info, *near, hg_own, hg_sib)


def plane_shift(first, by):
    pairs = []
    for x in range(4):
        for y in range(4):
            for core in range(2):
                along_x = (core == 0) == first
                to = ((x + by) % 4, y) if along_x else (x, (y + by) % 4)
                pairs.append(((x * 4 + y) * 2 + core, (to[0] * 4 + to[1]) * 2 + core))
    return pairs


def far_shift(by):
    return [(z, (z + 4 * by) % 16) for z in range(16)]


def column_shift(by):
    return [(z * 2 + c, (z + by[c]) % 16 * 2 + c) for z in range(16) for c in range(2)]


def second_axis_groups():
    place = [[[(x * 4 + y) * 2 + c for c in range(2)] for y in range(4)] for x in range(4)]
    along_y = [[place[j][i][0] for i in range(4)] for j in range(4)]
    along_x = [[place[i][j][1] for i in range(4)] for j in range(4)]
    return along_y + along_x


def first_axis_groups():
    place = [[[(x * 4 + y) * 2 + c for c in range(2)] for y in range(4)] for x in range(4)]
    along_x = [[place[i][j][0] for i in range(4)] for j in range(4)]
    along_y = [[place[j][i][1] for i in range(4)] for j in range(4)]
    return along_x + along_y


NEAR = ((1, 1), (2, -2), (-1, -1))


def per_device(inputs, weight, upstream, preactivation):
    core = lax.axis_index("core")
    info = jnp.stack([lax.axis_index(Z), core]).astype(jnp.int32)
    swap = [(0, 1), (1, 0)]

    slope = gelu_slope(preactivation.astype(jnp.float32))
    local = (upstream.astype(jnp.float32) * slope).astype(jnp.bfloat16)
    line = lax.all_gather(
        local, PLANE, axis=0, tiled=True, axis_index_groups=first_axis_groups()
    ).reshape(4, 32, 3072)
    inputs, line = lax.optimization_barrier((inputs, line))
    lines = lax.all_to_all(
        jnp.broadcast_to(line[None], (4, 4, 32, 3072)),
        PLANE,
        split_axis=0,
        concat_axis=0,
        tiled=True,
        axis_index_groups=second_axis_groups(),
    )
    near = [inputs] + [lax.ppermute(inputs, Z, far_shift(-d)) for d in (1, 2, 3)]
    lines, near = lax.optimization_barrier((lines, near))
    hg_own = lines.reshape(512, 3072)

    hg_sib = lax.ppermute(hg_own, "core", swap)
    sums = own_sums(hg_own, weight)
    own, *sends = sib_sums(info, sums, hg_sib, weight)
    own, near = lax.optimization_barrier((own, near))
    near = jnp.stack(near)
    nears = [near] + [lax.ppermute(near, Z + ("core",), column_shift(by)) for by in NEAR]
    received = [
        lax.ppermute(s, Z + ("core",), column_shift(by)) for s, by in zip(sends, NEAR)
    ]
    own, *sends = stage_sums(info, own, received)
    far = [lax.ppermute(s, Z, far_shift(d + 1)) for d, s in enumerate(sends)]
    weight_total = weight_sums(info, nears, hg_own, hg_sib)
    weight_total, *far = lax.optimization_barrier((weight_total, *far))
    return (final_sums(own, far), weight_total)


def solution(mesh):
    fine = Mesh(
        mesh.devices.reshape(4, 2, 4, 4, 2, 2), ("x", "yh", "zh", "zl", "yl", "core")
    )
    in_specs = (P(Z, PLANE), P(PLANE, Z), P(PLANE, Z), P(PLANE, Z))
    out_specs = (P(Z, PLANE), P(PLANE, Z))
    return jax.shard_map(
        per_device, mesh=fine, in_specs=in_specs, out_specs=out_specs, check_vma=False
    )
```
